512 devices in a mesh: member: 16 (over y, x_lo, core), node: 32 (over z, x_hi).
Axes of the slice: x: 4 (x_hi: 2, x_lo: 2; x = x_hi * 2 + x_lo), y: 4, z: 16, core: 2. Of those that a mesh axis runs over, the one named last changes fastest.
Arguments:
- latent: bfloat16 [8192, 1024], P('node', 'member'), may hold values from -6 to 6
- member_perturbations: bfloat16 [16, 8192, 1024], P('member', 'node'), may hold values from -12 to 12
- layer_norm_gain: bfloat16 [1024], replicated, may hold values from 0.099609375 to 1.8984375
- query_key_value_weight: bfloat16 [1024, 1536], P('node'), may hold values from -0.1875 to 0.1875
- output_weight_matrix: bfloat16 [512, 1024], P('node'), may hold values from -0.25 to 0.25
- decoder_weight_matrix: bfloat16 [98, 1024], replicated, may hold values from -0.1875 to 0.1875
- observed_truth: float32 [98, 8192], P(None, 'node'), may hold values from -9 to 9
- region_mask: int32 [8192], P('node'), may hold values from 0 to 1, as said below
- node_window_halfspan: int32 [8192], P('node'), may hold values from 64 to 256, as said below
Outputs:
- loss: float32 [], replicated
- latent_grad: float32 [8192, 1024], P('node', 'member')
- noise_grad: float32 [16, 8192, 1024], P('member', 'node')
The draws below stay inside these ranges and needn't reach their ends.
Inputs may be any that keep to these rules, and one draw needn't show every extreme that they name: `region_mask`: 1 on one contiguous run of 2048 nodes whose start is drawn, 0 on all other nodes. `node_window_halfspan`: equal to 256 on every node of the region.
All inputs are finite; a program needn't handle non-finite values.
Results may differ from the reference program's by a relative error of at most 0.019.
Values may be sent and summed in bfloat16 or wider, within the bound.
No kernel may reach another device: no remote copies, remote signals or barrier semaphores. Data moves between devices by JAX's collectives and lax.ppermute only.
A program may use at most 64 MiB of HBM per device.

```python
import jax
import jax.numpy as jnp
from jax import lax

D = 1024
HEADS = 8
VARS = 98
HALF = 256
REACH_MIN = 64
NODE_DEV = 256
INNER = 512
REALIZATIONS = 16
NODES = 8192
N_NODE = 32


def region_start(key):
    return jax.random.randint(key, (), 0, NODES - NODES // 4 + 1)


def draw_region_mask(key, part):
    first_node = region_start(key)
    position = jnp.arange(NODES, dtype=jnp.int32)
    inside = (position >= first_node) & (position < first_node + NODES // 4)
    return inside.astype(jnp.int32)


def draw_node_window_halfspan(key, part):
    first_node = region_start(key)
    other_key = jax.random.fold_in(key, 5)
    position = jnp.arange(NODES, dtype=jnp.int32)
    inside = (position >= first_node) & (position < first_node + NODES // 4)
    dispersion_amount = jax.random.randint(other_key, (NODES,), REACH_MIN, HALF + 1)
    return jnp.where(inside, HALF, dispersion_amount).astype(jnp.int32)


def member_scales(lowest, ratio):
    ladder = jnp.arange(REALIZATIONS, dtype=jnp.float32) / (REALIZATIONS - 1)
    return (lowest * ratio ** ladder)[:, None, None]


def draw_member_perturbations(key, part):
    key = jax.random.fold_in(key, 11)
    values = jax.random.truncated_normal(key, -4.0, 4.0, (REALIZATIONS, NODES, D), jnp.float32)
    values = values * member_scales(0.5, 6.0)
    return values.astype(jnp.bfloat16)


def levels(own_key, dims, cuts, least, top_value):
    def one(axis_at, shards_of):
        heights = jax.random.uniform(jax.random.fold_in(jax.random.fold_in(own_key, 6), axis_at), (shards_of,), jnp.float32, least / len(cuts), top_value / len(cuts))
        return jnp.repeat(jnp.exp(heights), dims[axis_at] // shards_of).reshape((-1,) + (1,) * (len(dims) - axis_at - 1))

    loudness = one(*cuts[0])
    for cut in cuts[1:]:
        loudness = loudness * one(*cut)
    return loudness


def bell_draw(key, shape, scale, most, cuts=(), kind=jnp.bfloat16):
    values = jax.random.normal(key, shape, jnp.float32) * scale
    if len(cuts) > 0:
        values = levels(key, shape, cuts, -0.22, 0.18) * values
    return jnp.clip(values, min=-most, max=most).astype(kind)


def setup_inputs(seed: int = 0) -> dict:
    streams_of = jax.random.split(jax.random.key(seed), 10)
    latent = bell_draw(streams_of[0], (NODES, D), 1.0, 6.0, ((0, 32), (1, 16)))
    member_perturbations = draw_member_perturbations(jax.random.fold_in(streams_of[9], 71), 0)
    layer_norm_gain = jnp.clip(1.0 + 0.18 * jax.random.normal(streams_of[2], (D,), jnp.float32), 0.099609375, 1.8984375).astype(jnp.bfloat16)
    query_key_value_weight = bell_draw(streams_of[3], (D, 3 * INNER), D ** -0.5, 0.1875, ((0, 32),))
    output_weight_matrix = bell_draw(streams_of[4], (INNER, D), INNER ** -0.5, 0.25, ((0, 32),))
    decoder_weight_matrix = bell_draw(streams_of[5], (VARS, D), D ** -0.5, 0.1875)
    observed_truth = bell_draw(streams_of[6], (VARS, NODES), 1.5, 9.0, ((1, 32),), jnp.float32)
    region_mask = draw_region_mask(jax.random.fold_in(streams_of[9], 71), 0)
    node_window_halfspan = draw_node_window_halfspan(jax.random.fold_in(streams_of[9], 71), 0)
    return {"latent": latent, "member_perturbations": member_perturbations, "layer_norm_gain": layer_norm_gain, "query_key_value_weight": query_key_value_weight, "output_weight_matrix": output_weight_matrix, "decoder_weight_matrix": decoder_weight_matrix, "observed_truth": observed_truth, "region_mask": region_mask, "node_window_halfspan": node_window_halfspan}


norm_epsilon = 1e-05
head_epsilon = 1e-06
smooth_width = 0.1
region_share = 0.25

def contract_trailing_axis(left, right):
    return lax.dot_general(left, right, (((1,), (1,)), ((), ())), preferred_element_type=jnp.float32)

def contract_first(left, right):
    return lax.dot_general(left, right, (((0,), (0,)), ((), ())), preferred_element_type=jnp.float32)

def layer_norm(hidden_state):
    average = lax.optimization_barrier(jnp.mean(hidden_state, axis=1, keepdims=True))
    centred = hidden_state - average
    inverse = lax.rsqrt(lax.optimization_barrier(jnp.mean(centred * centred, axis=1, keepdims=True)) + norm_epsilon)
    return (centred * inverse, inverse)

def layer_norm_back(standard, inverse, loss_derivative):
    first_term = lax.optimization_barrier(jnp.mean(loss_derivative, axis=1, keepdims=True))
    second_term = standard * lax.optimization_barrier(jnp.mean(loss_derivative * standard, axis=1, keepdims=True))
    return inverse * (loss_derivative - first_term - second_term)

def head_norm(block_rows, head_count):
    row_count = block_rows.shape[0]
    per_head = block_rows.reshape(row_count, head_count, -1)
    inverse = lax.rsqrt(lax.optimization_barrier(jnp.mean(per_head * per_head, axis=2, keepdims=True)) + head_epsilon)
    return ((per_head * inverse).reshape(row_count, -1), inverse)

def head_norm_back(unit_rows, inverse, upstream, head_count):
    row_count = unit_rows.shape[0]
    unit_heads = unit_rows.reshape(row_count, head_count, -1)
    up_heads = upstream.reshape(row_count, head_count, -1)
    along = lax.optimization_barrier(jnp.mean(up_heads * unit_heads, axis=2, keepdims=True))
    return (inverse * (up_heads - unit_heads * along)).reshape(row_count, -1)

def window_mask(row_start, node_window_halfspan, node_total, half_window):
    row_count = node_window_halfspan.shape[0]
    query_pos = row_start + jnp.arange(row_count, dtype=jnp.int32)[:, None]
    key_pos = row_start - half_window + jnp.arange(row_count + 2 * half_window, dtype=jnp.int32)[None, :]
    offset = key_pos - query_pos
    inside = (offset >= -node_window_halfspan[:, None]) & (offset < node_window_halfspan[:, None])
    return inside & (key_pos >= 0) & (key_pos < node_total)

def head_weights(q_head, k_head, allowed, factor):
    exponent = jnp.where(allowed, jnp.exp(contract_trailing_axis(q_head, k_head) * factor), 0.0)
    return exponent / lax.optimization_barrier(jnp.sum(exponent, axis=1, keepdims=True))

def attend(q_norm, kv_ext, allowed, head_count):
    inner_width = q_norm.shape[1]
    head_size = inner_width // head_count
    factor = head_size ** (-0.5)

    def one_head(head_index, mixed):
        head_start = head_index * head_size
        q_head = lax.dynamic_slice_in_dim(q_norm, head_start, head_size, 1)
        k_head = lax.dynamic_slice_in_dim(kv_ext, head_start, head_size, 1)
        v_head = lax.dynamic_slice_in_dim(kv_ext, inner_width + head_start, head_size, 1)
        probabilities = head_weights(q_head, k_head, allowed, factor).astype(jnp.bfloat16)
        result = jnp.dot(probabilities, v_head, preferred_element_type=jnp.float32).astype(jnp.bfloat16)
        return lax.dynamic_update_slice_in_dim(mixed, result, head_start, 1)
    return lax.fori_loop(0, head_count, one_head, jnp.zeros(q_norm.shape, jnp.bfloat16))

def attend_back(q_norm, kv_ext, allowed, mixed_grad, head_count):
    inner_width = q_norm.shape[1]
    head_size = inner_width // head_count
    factor = head_size ** (-0.5)

    def one_head(head_index, state_pair):
        q_grad, kv_grad = state_pair
        head_start = head_index * head_size
        q_head = lax.dynamic_slice_in_dim(q_norm, head_start, head_size, 1)
        k_head = lax.dynamic_slice_in_dim(kv_ext, head_start, head_size, 1)
        v_head = lax.dynamic_slice_in_dim(kv_ext, inner_width + head_start, head_size, 1)
        out_grad = lax.dynamic_slice_in_dim(mixed_grad, head_start, head_size, 1)
        weights = head_weights(q_head, k_head, allowed, factor)
        probabilities = weights.astype(jnp.bfloat16)
        weight_grad = contract_trailing_axis(out_grad, v_head)
        row_dot = lax.optimization_barrier(jnp.sum(weights * weight_grad, axis=1, keepdims=True))
        score_grad = (weights * (weight_grad - row_dot) * factor).astype(jnp.bfloat16)
        q_part = jnp.dot(score_grad, k_head, preferred_element_type=jnp.float32)
        k_part = contract_first(score_grad, q_head)
        v_part = contract_first(probabilities, out_grad)
        q_grad = lax.dynamic_update_slice_in_dim(q_grad, q_part, head_start, 1)
        kv_grad = lax.dynamic_update_slice_in_dim(kv_grad, k_part, head_start, 1)
        kv_grad = lax.dynamic_update_slice_in_dim(kv_grad, v_part, inner_width + head_start, 1)
        return (q_grad, kv_grad)
    start_pair = (jnp.zeros(q_norm.shape, jnp.float32), jnp.zeros(kv_ext.shape, jnp.float32))
    return lax.fori_loop(0, head_count, one_head, start_pair)

def softened_magnitude(difference):
    return jnp.sqrt(difference * difference + smooth_width * smooth_width)

def softened_derivative(difference):
    return difference / softened_magnitude(difference)

def member_forward_pass(hidden_state, layer_norm_gain, query_key_value_weight, output_weight_matrix, decoder_weight_matrix, node_window_halfspan):
    standard, inverse = layer_norm(hidden_state)
    normed = (standard * layer_norm_gain.astype(jnp.float32)).astype(jnp.bfloat16)
    projected = jnp.dot(normed, query_key_value_weight, preferred_element_type=jnp.float32)
    q_unit, q_inverse = head_norm(projected[:, :INNER], HEADS)
    k_unit, k_inverse = head_norm(projected[:, INNER:2 * INNER], HEADS)
    q_norm = q_unit.astype(jnp.bfloat16)
    key_value = jnp.concatenate([k_unit.astype(jnp.bfloat16), projected[:, 2 * INNER:].astype(jnp.bfloat16)], axis=1)
    padded = jnp.pad(key_value, ((HALF, HALF), (0, 0)))

    def one_block(block_index):
        row_start = block_index * NODE_DEV
        q_block = lax.dynamic_slice_in_dim(q_norm, row_start, NODE_DEV, 0)
        kv_block = lax.dynamic_slice_in_dim(padded, row_start, NODE_DEV + 2 * HALF, 0)
        reach_block = lax.dynamic_slice_in_dim(node_window_halfspan, row_start, NODE_DEV, 0)
        allowed = window_mask(row_start, reach_block, NODES, HALF)
        return attend(q_block, kv_block, allowed, HEADS)
    mixed = lax.map(one_block, jnp.arange(N_NODE, dtype=jnp.int32)).reshape(NODES, INNER)
    updated_state = (hidden_state + jnp.dot(mixed, output_weight_matrix, preferred_element_type=jnp.float32)).astype(jnp.bfloat16)
    realization_outlook = contract_trailing_axis(decoder_weight_matrix, updated_state)
    saved_residuals = (standard, inverse, q_unit, q_inverse, k_unit, k_inverse, q_norm, padded)
    return (realization_outlook, saved_residuals)

def backward_member(hidden_state, pred_grad, layer_norm_gain, query_key_value_weight, output_weight_matrix, decoder_weight_matrix, node_window_halfspan):
    realization_outlook, saved_residuals = member_forward_pass(hidden_state, layer_norm_gain, query_key_value_weight, output_weight_matrix, decoder_weight_matrix, node_window_halfspan)
    standard, inverse, q_unit, q_inverse, k_unit, k_inverse, q_norm, padded = saved_residuals
    upd_grad = contract_first(pred_grad, decoder_weight_matrix)
    mixed_grad = contract_trailing_axis(upd_grad.astype(jnp.bfloat16), output_weight_matrix).astype(jnp.bfloat16)

    def one_block(pad_grad, block_index):
        row_start = block_index * NODE_DEV
        q_block = lax.dynamic_slice_in_dim(q_norm, row_start, NODE_DEV, 0)
        kv_block = lax.dynamic_slice_in_dim(padded, row_start, NODE_DEV + 2 * HALF, 0)
        reach_block = lax.dynamic_slice_in_dim(node_window_halfspan, row_start, NODE_DEV, 0)
        grad_block = lax.dynamic_slice_in_dim(mixed_grad, row_start, NODE_DEV, 0)
        allowed = window_mask(row_start, reach_block, NODES, HALF)
        q_part, kv_part = attend_back(q_block, kv_block, allowed, grad_block, HEADS)
        current = lax.dynamic_slice_in_dim(pad_grad, row_start, NODE_DEV + 2 * HALF, 0)
        pad_grad = lax.dynamic_update_slice_in_dim(pad_grad, current + kv_part, row_start, 0)
        return (pad_grad, q_part)
    pad_start = jnp.zeros((NODES + 2 * HALF, 2 * INNER), jnp.float32)
    pad_grad, q_blocks = lax.scan(one_block, pad_start, jnp.arange(N_NODE, dtype=jnp.int32))
    q_grad = q_blocks.reshape(NODES, INNER)
    kv_grad = pad_grad[HALF:HALF + NODES]
    q_raw = head_norm_back(q_unit, q_inverse, q_grad, HEADS)
    k_raw = head_norm_back(k_unit, k_inverse, kv_grad[:, :INNER], HEADS)
    qkv_grad = jnp.concatenate([q_raw, k_raw, kv_grad[:, INNER:]], axis=1).astype(jnp.bfloat16)
    normed_grad = contract_trailing_axis(qkv_grad, query_key_value_weight)
    return upd_grad + layer_norm_back(standard, inverse, normed_grad * layer_norm_gain.astype(jnp.float32))

def reference(latent, member_perturbations, layer_norm_gain, query_key_value_weight, output_weight_matrix, decoder_weight_matrix, observed_truth, region_mask, node_window_halfspan):
    base = latent.astype(jnp.float32)

    def single_member_prediction(perturbation_rows):
        hidden_state = base + perturbation_rows.astype(jnp.float32)
        return member_forward_pass(hidden_state, layer_norm_gain, query_key_value_weight, output_weight_matrix, decoder_weight_matrix, node_window_halfspan)[0]
    ensemble_predictions = lax.map(single_member_prediction, member_perturbations)
    cell_surface_factor = 1.0 - (1.0 - region_share) * region_mask.astype(jnp.float32)

    def member_score_terms(shard_gridpoint_entries):
        mutual_separations = shard_gridpoint_entries[None] - ensemble_predictions
        misfit_vs_truth = shard_gridpoint_entries - observed_truth
        loss_derivative = softened_derivative(misfit_vs_truth) - lax.optimization_barrier(jnp.sum(softened_derivative(mutual_separations), axis=0)) / (REALIZATIONS - 1)
        dispersion_amount = (lax.optimization_barrier(jnp.sum(softened_magnitude(mutual_separations), axis=0)) - smooth_width) / (2 * (REALIZATIONS - 1))
        incomplete_crps_sum = jnp.sum(cell_surface_factor * (softened_magnitude(misfit_vs_truth) - dispersion_amount))
        return ((cell_surface_factor * loss_derivative).astype(jnp.bfloat16), incomplete_crps_sum)
    prediction_gradients, partial_results = lax.map(member_score_terms, ensemble_predictions)
    loss = jnp.sum(partial_results) / (REALIZATIONS * NODES * VARS)

    def member_back(running, inputs):
        perturbation_rows, pred_grad = inputs
        hidden_state = base + perturbation_rows.astype(jnp.float32)
        hidden_grad = backward_member(hidden_state, pred_grad, layer_norm_gain, query_key_value_weight, output_weight_matrix, decoder_weight_matrix, node_window_halfspan)
        return (running + hidden_grad, hidden_grad)
    running, noise_grad = lax.scan(member_back, jnp.zeros((NODES, D), jnp.float32), (member_perturbations, prediction_gradients))
    return (loss, running, noise_grad)
```

```python
import functools
import math

import jax
import jax.numpy as jnp
from jax import lax
from jax.experimental import pallas as pl
from jax.experimental.pallas import tpu as pltpu
from jax.sharding import Mesh, PartitionSpec as P

HEADS = 8
HEAD = 64
INNER = 512
ROWS = 256
HALF = 256
EXT = ROWS + 2 * HALF
WIDTH = 1024
VARS = 98
LANES = 128
MEMBERS = 16
SLOT = ROWS // MEMBERS
TILE = 128
WINDOW = TILE + 2 * HALF
PACKED = 2048

norm_epsilon = 1e-05
head_epsilon = 1e-06
smooth_width = 0.1
region_share = 0.25
exponent_scale = math.log2(math.e) / 8.0

MEMBER = ("y", "xl", "c")
NODE = ("z", "xh")
EVERY = MEMBER + NODE

bf16 = jnp.bfloat16
f32 = jnp.float32


def mm(left, right):
    return lax.dot_general(left, right, (((1,), (0,)), ((), ())), preferred_element_type=f32)


def mm_t(left, right):
    return lax.dot_general(left, right, (((1,), (1,)), ((), ())), preferred_element_type=f32)


def split(value):
    high = value.astype(bf16)
    return high, (value - high.astype(f32)).astype(bf16)


def segment_matrix(scale):
    rows = lax.broadcasted_iota(jnp.int32, (INNER, INNER), 0) // HEAD
    columns = lax.broadcasted_iota(jnp.int32, (INNER, INNER), 1) // HEAD
    return jnp.where(rows == columns, scale, 0.0).astype(bf16)


def head_sums(value, segments):
    high, low = split(value)
    return mm(high, segments) + mm(low, segments)


def lane_index(rows, lanes):
    return lax.broadcasted_iota(jnp.int32, (rows, lanes), 1)


def norm_kernel(lat_ref, low_ref, own_ref, high_ref, gain_ref, normed_ref, latent_ref):
    gain = gain_ref[...].astype(f32)
    for block, pert_ref in enumerate((low_ref, own_ref, high_ref)):
        for part in range(2):
            rows = slice(part * TILE, (part + 1) * TILE)
            lanes = slice(block * ROWS + part * TILE, block * ROWS + (part + 1) * TILE)
            lat = lat_ref[:, lanes].astype(f32).T
            if block == 1:
                latent_ref[rows, :] = lat.astype(bf16)
            hidden = lat + pert_ref[rows, :].astype(f32)
            centred = hidden - jnp.mean(hidden, axis=1, keepdims=True)
            inverse = lax.rsqrt(jnp.mean(centred * centred, axis=1, keepdims=True) + norm_epsilon)
            normed_ref[lanes, :] = (centred * inverse * gain).astype(bf16)


def out_weights(w_ref, side):
    rows = slice(side * 16, side * 16 + 16)
    return w_ref[:, rows, 3 * INNER :].reshape(INNER // 2, INNER)


def qkv_weights(w_ref, part):
    return w_ref[:, :, part * INNER : (part + 1) * INNER].reshape(INNER, INNER)


def forward_kernel(
    place_ref, normed_ref, wa_ref, wb_ref, latent_ref, pert_ref, reach_ref, decoder_ref,
    q_ref, k_ref, v_ref, unit_ref, factor_ref, mixed_ref, total_ref, forecast_ref,
    bias_ref, mixed_low_ref,
):
    core = place_ref[0]
    row_start = place_ref[1]
    segments = segment_matrix(1.0 / HEAD)
    near = pl.ds(pl.multiple_of(core * INNER, INNER), INNER)
    far = pl.ds(pl.multiple_of((1 - core) * INNER, INNER), INNER)
    for block in range(3):
        rows = slice(block * ROWS, (block + 1) * ROWS)
        left, right = normed_ref[rows, near], normed_ref[rows, far]
        for part, out_ref in enumerate((q_ref, k_ref, v_ref)):
            projected = mm(left, qkv_weights(wa_ref, part)) + mm(right, qkv_weights(wb_ref, part))
            if part < 2:
                factor = lax.rsqrt(head_sums(projected * projected, segments) + head_epsilon)
                unit = projected * factor
                if block == 1:
                    unit_ref[:, part * INNER : (part + 1) * INNER] = unit
                    factor_ref[:, part * INNER : (part + 1) * INNER] = factor
                projected = unit
            out_ref[rows, :] = projected.astype(bf16)

    for tile in range(2):
        offset = (
            lane_index(TILE, WINDOW)
            - HALF
            - lax.broadcasted_iota(jnp.int32, (TILE, WINDOW), 0)
        )
        position = row_start - HALF + tile * TILE + lane_index(TILE, WINDOW)
        reach = reach_ref[tile * TILE : (tile + 1) * TILE, :]
        inside = (offset >= -reach) & (offset < reach) & (position >= 0) & (position < place_ref[2])
        bias_ref[tile] = jnp.where(inside, 0.0, -1e30)

    first = lane_index(1, LANES) < HEAD

    def one_pair(pair, carry):
        lanes = pl.ds(pl.multiple_of(pair * LANES, LANES), LANES)
        for tile in range(2):
            rows = slice(tile * TILE, (tile + 1) * TILE)
            window = slice(tile * TILE, tile * TILE + WINDOW)
            queries = q_ref[ROWS + tile * TILE : ROWS + (tile + 1) * TILE, lanes]
            keys = k_ref[window, lanes]
            values = v_ref[window, lanes]
            bias = bias_ref[tile]
            outs = []
            for mine in (first, ~first):
                score = mm_t(jnp.where(mine, queries, jnp.zeros_like(queries)), keys)
                weight = jnp.exp2(score * exponent_scale + bias).astype(bf16)
                outs.append(mm(weight, jnp.where(mine, values, jnp.ones_like(values))))
            total = pltpu.roll(jnp.where(first, outs[1], outs[0]), HEAD, 1)
            mixed = jnp.where(first, outs[0], outs[1]) / total
            mixed_ref[rows, lanes] = mixed
            mixed_low_ref[rows, lanes] = mixed.astype(bf16)
            total_ref[rows, lanes] = total
        return carry

    lax.fori_loop(0, HEADS // 2, one_pair, 0)

    near_out = pl.ds(pl.multiple_of(core * (INNER // 2), INNER // 2), INNER // 2)
    far_out = pl.ds(pl.multiple_of((1 - core) * (INNER // 2), INNER // 2), INNER // 2)
    left, right = mixed_low_ref[:, near_out], mixed_low_ref[:, far_out]
    forecast = jnp.zeros((ROWS, LANES), f32)
    for side in range(2):
        columns = slice(side * INNER, (side + 1) * INNER)
        branch = mm(left, out_weights(wa_ref, side)) + mm(right, out_weights(wb_ref, side))
        hidden = latent_ref[:, columns].astype(f32) + pert_ref[:, columns].astype(f32)
        updated = (hidden + branch).astype(bf16)
        forecast = forecast + mm_t(updated, decoder_ref[:, columns])
    forecast_ref[...] = forecast


def score_kernel(forecast_ref, truth_ref, area_ref, out_ref):
    lanes = lane_index(SLOT, LANES)
    area = jnp.where(lanes < VARS, area_ref[...], 0.0)
    truth = truth_ref[...]
    square = smooth_width * smooth_width
    loss = jnp.zeros((SLOT, LANES), f32)
    for member in range(MEMBERS):
        own = forecast_ref[member]
        pull = jnp.zeros((SLOT, LANES), f32)
        spread = jnp.zeros((SLOT, LANES), f32)
        for other in range(MEMBERS):
            if other == member:
                continue
            gap = own - forecast_ref[other]
            power = gap * gap + square
            inverse = lax.rsqrt(power)
            pull = pull + gap * inverse
            spread = spread + power * inverse
        gap = own - truth
        power = gap * gap + square
        inverse = lax.rsqrt(power)
        loss = loss + area * (power * inverse - spread * (0.5 / (MEMBERS - 1)))
        out_ref[member] = (area * (gap * inverse - pull * (1.0 / (MEMBERS - 1)))).astype(bf16)
    total = jnp.sum(jnp.sum(loss, axis=1, keepdims=True), axis=0, keepdims=True)
    total = jnp.broadcast_to(total, (SLOT, LANES))
    high, rest = split(total)
    middle = rest
    low = (total - high.astype(f32) - middle.astype(f32)).astype(bf16)
    for member in range(MEMBERS):
        kept = out_ref[member]
        kept = jnp.where(lanes == VARS, high, kept)
        kept = jnp.where(lanes == VARS + 1, middle, kept)
        out_ref[member] = jnp.where(lanes == VARS + 2, low, kept)


def mixed_gradient(upd_low, core, wa_ref, wb_ref, target_ref, rows):
    near_out = pl.ds(pl.multiple_of(core * (INNER // 2), INNER // 2), INNER // 2)
    far_out = pl.ds(pl.multiple_of((1 - core) * (INNER // 2), INNER // 2), INNER // 2)
    for w_ref, lanes in ((wa_ref, near_out), (wb_ref, far_out)):
        target_ref[rows, lanes] = mm_t(upd_low[:, :INNER], out_weights(w_ref, 0)) + mm_t(
            upd_low[:, INNER:], out_weights(w_ref, 1)
        )


def gradient_operands(scaled, row_dot, g0_ref, g1_ref, rows):
    first = lane_index(1, LANES) < HEAD
    spot = lane_index(ROWS, LANES) % HEAD
    for pair in range(HEADS // 2):
        lanes = slice(pair * LANES, (pair + 1) * LANES)
        high, low = split(-pltpu.roll(row_dot[:, lanes], HEAD, 1))
        zero = jnp.zeros_like(high)
        extra = jnp.where(spot == 0, high, jnp.where(spot == 1, low, zero))
        own = scaled[:, lanes]
        g0_ref[rows, lanes] = jnp.where(first, own, extra)
        g1_ref[rows, lanes] = jnp.where(first, extra, own)


def pick(base, rows, lanes):
    row = lax.broadcasted_iota(jnp.int32, (rows, lanes), 0)
    lane = lane_index(rows, lanes)
    return row, lane


def upstream_kernel(
    place_ref, pg_ref, decoder_ref, wa_ref, wb_ref, mixed_ref, total_ref,
    upd_ref, scaled_ref, g0_ref, g1_ref, message_ref, loss_ref, grad_ref,
):
    core = place_ref[0]
    pg = pg_ref[...]
    upd = mm(pg, decoder_ref[...])
    upd_ref[...] = upd
    everything = slice(0, ROWS)
    mixed_gradient(upd.astype(bf16), core, wa_ref, wb_ref, grad_ref, everything)
    grad = grad_ref[...].astype(bf16).astype(f32)
    total = total_ref[...]
    inverse = 1.0 / total
    row_dot = head_sums(grad * mixed_ref[...], segment_matrix(1.0)) * inverse
    scaled = (grad * inverse).astype(bf16)
    scaled_ref[...] = scaled
    gradient_operands(scaled, row_dot, g0_ref, g1_ref, everything)

    row, lane = pick(None, INNER, LANES)
    head_row = (row % HEAD == 0)
    chosen = lambda start: jnp.where(head_row & (lane == start + row // HEAD), 1.0, 0.0).astype(bf16)
    high, low = split(total)
    stats = mm(high, chosen(VARS)) + mm(low, chosen(VARS + 8)) + mm(row_dot.astype(bf16), chosen(VARS + 16))
    lanes = lane_index(ROWS, LANES)
    message_ref[...] = jnp.where(lanes < VARS, pg.astype(f32), stats).astype(bf16)
    kept = jnp.where((lanes >= VARS) & (lanes < VARS + 3), pg.astype(f32), 0.0)
    total_loss = jnp.sum(jnp.sum(kept, axis=1, keepdims=True), axis=0, keepdims=True) * (1.0 / SLOT)
    loss_ref[...] = jnp.broadcast_to(total_loss, (8, LANES))


def query_kernel(
    place_ref, q_ref, k_ref, v_ref, g0_ref, g1_ref, reach_ref, qgrad_ref, bias_ref,
):
    row_start = place_ref[1]
    for tile in range(2):
        offset = (
            lane_index(TILE, WINDOW)
            - HALF
            - lax.broadcasted_iota(jnp.int32, (TILE, WINDOW), 0)
        )
        position = row_start - HALF + tile * TILE + lane_index(TILE, WINDOW)
        reach = reach_ref[tile * TILE : (tile + 1) * TILE, :]
        inside = (offset >= -reach) & (offset < reach) & (position >= 0) & (position < place_ref[2])
        bias_ref[tile] = jnp.where(inside, 0.0, -1e30)
    first = lane_index(1, LANES) < HEAD

    def one_pair(pair, carry):
        lanes = pl.ds(pl.multiple_of(pair * LANES, LANES), LANES)
        for tile in range(2):
            rows = slice(tile * TILE, (tile + 1) * TILE)
            window = slice(tile * TILE, tile * TILE + WINDOW)
            queries = q_ref[ROWS + tile * TILE : ROWS + (tile + 1) * TILE, lanes]
            keys = k_ref[window, lanes]
            values = v_ref[window, lanes]
            bias = bias_ref[tile]
            grads = []
            for mine, g_ref in ((first, g0_ref), (~first, g1_ref)):
                score = mm_t(jnp.where(mine, queries, jnp.zeros_like(queries)), keys)
                weight = jnp.exp2(score * exponent_scale + bias)
                pull = mm_t(g_ref[rows, lanes], jnp.where(mine, values, jnp.ones_like(values)))
                grads.append(mm((weight * pull).astype(bf16), keys))
            qgrad_ref[rows, lanes] = jnp.where(first, grads[0], grads[1]) * 0.125
        return carry

    lax.fori_loop(0, HEADS // 2, one_pair, 0)


def backward_kernel(
    place_ref, low_ref, high_ref, decoder_ref, wa_ref, wb_ref, q_ref, k_ref, v_ref,
    scaled_ref, g0_ref, g1_ref, reach_ref, qgrad_ref, unit_ref, factor_ref,
    latent_ref, pert_ref, gain_ref, upd_ref, loss_a_ref, loss_b_ref,
    noise_ref, send_ref,
    all_scaled, all_g0, all_g1, bias_ref, grad_ref, kv_ref, normed_grad_ref,
):
    core = place_ref[0]
    row, lane = pick(None, LANES, INNER)
    spread = lambda start: row == start + lane // HEAD
    expand_total = jnp.where(spread(VARS) | spread(VARS + 8), 1.0, 0.0).astype(bf16)
    expand_dot = jnp.where(spread(VARS + 16), 1.0, 0.0).astype(bf16)
    middle = slice(ROWS, 2 * ROWS)
    all_scaled[middle, :] = scaled_ref[...]
    all_g0[middle, :] = g0_ref[...]
    all_g1[middle, :] = g1_ref[...]
    for block, message_ref in ((0, low_ref), (2, high_ref)):
        rows = slice(block * ROWS, (block + 1) * ROWS)
        message = message_ref[...]
        mixed_gradient(mm(message, decoder_ref[...]).astype(bf16), core, wa_ref, wb_ref, grad_ref, slice(0, ROWS))
        grad = grad_ref[...].astype(bf16).astype(f32)
        total = mm(message, expand_total)
        scaled = (grad / jnp.where(total > 0.0, total, 1.0)).astype(bf16)
        all_scaled[rows, :] = scaled
        gradient_operands(scaled, mm(message, expand_dot), all_g0, all_g1, rows)

    for tile in range(2):
        offset = (
            HALF
            + lax.broadcasted_iota(jnp.int32, (TILE, WINDOW), 0)
            - lane_index(TILE, WINDOW)
        )
        reach = reach_ref[0:1, tile * TILE : tile * TILE + WINDOW]
        bias_ref[tile] = jnp.where((offset >= -reach) & (offset < reach), 0.0, -1e30)
    first = lane_index(1, LANES) < HEAD

    def one_pair(pair, carry):
        start = pl.multiple_of(pair * LANES, LANES)
        lanes = pl.ds(start, LANES)
        value_lanes = pl.ds(pl.multiple_of(INNER + start, LANES), LANES)
        for tile in range(2):
            rows = slice(tile * TILE, (tile + 1) * TILE)
            window = slice(tile * TILE, tile * TILE + WINDOW)
            keys = k_ref[ROWS + tile * TILE : ROWS + (tile + 1) * TILE, lanes]
            values = v_ref[ROWS + tile * TILE : ROWS + (tile + 1) * TILE, lanes]
            queries = q_ref[window, lanes]
            scaled = all_scaled[window, lanes]
            bias = bias_ref[tile]
            key_grads = []
            value_grads = []
            for mine, g_ref in ((first, all_g0), (~first, all_g1)):
                score = mm_t(jnp.where(mine, keys, jnp.zeros_like(keys)), queries)
                weight = jnp.exp2(score * exponent_scale + bias)
                pull = mm_t(jnp.where(mine, values, jnp.ones_like(values)), g_ref[window, lanes])
                value_grads.append(mm(weight.astype(bf16), scaled))
                key_grads.append(mm((weight * pull).astype(bf16), queries))
            kv_ref[rows, lanes] = jnp.where(first, key_grads[0], key_grads[1]) * 0.125
            kv_ref[rows, value_lanes] = jnp.where(first, value_grads[0], value_grads[1])
        return carry

    lax.fori_loop(0, HEADS // 2, one_pair, 0)

    segments = segment_matrix(1.0 / HEAD)
    parts = []
    for part, grad in ((0, qgrad_ref[...]), (1, kv_ref[:, :INNER])):
        columns = slice(part * INNER, (part + 1) * INNER)
        unit = unit_ref[:, columns]
        along = head_sums(grad * unit, segments)
        parts.append((factor_ref[:, columns] * (grad - unit * along)).astype(bf16))
    parts.append(kv_ref[:, INNER:].astype(bf16))
    near = pl.ds(pl.multiple_of(core * INNER, INNER), INNER)
    far = pl.ds(pl.multiple_of((1 - core) * INNER, INNER), INNER)
    for w_ref, lanes in ((wa_ref, near), (wb_ref, far)):
        normed_grad_ref[:, lanes] = (
            mm_t(parts[0], qkv_weights(w_ref, 0))
            + mm_t(parts[1], qkv_weights(w_ref, 1))
            + mm_t(parts[2], qkv_weights(w_ref, 2))
        )
    gain = gain_ref[...].astype(f32)
    for part in range(2):
        rows = slice(part * TILE, (part + 1) * TILE)
        hidden = latent_ref[rows, :].astype(f32) + pert_ref[rows, :].astype(f32)
        centred = hidden - jnp.mean(hidden, axis=1, keepdims=True)
        inverse = lax.rsqrt(jnp.mean(centred * centred, axis=1, keepdims=True) + norm_epsilon)
        standard = centred * inverse
        grad = normed_grad_ref[rows, :] * gain
        first_term = jnp.mean(grad, axis=1, keepdims=True)
        second_term = standard * jnp.mean(grad * standard, axis=1, keepdims=True)
        result = upd_ref[rows, :] + inverse * (grad - first_term - second_term)
        noise_ref[rows, :] = result
        turned = result.T.astype(bf16)
        for member in range(MEMBERS):
            send_ref[member, :HEAD, rows] = turned[member * HEAD : (member + 1) * HEAD, :]
    loss = jnp.broadcast_to(loss_a_ref[0:1, 0:1] + loss_b_ref[0:1, 0:1], (16, ROWS))
    high, mid = split(loss)
    low = (loss - high.astype(f32) - mid.astype(f32)).astype(bf16)
    lanes = lane_index(16, ROWS)
    tail = jnp.where(lanes == 0, high, jnp.where(lanes == 1, mid, jnp.where(lanes == 2, low, jnp.zeros_like(low))))
    for member in range(MEMBERS):
        send_ref[member, HEAD:, :] = tail


def finish_kernel(received_ref, latent_grad_ref, loss_ref):
    total = received_ref[0].astype(f32)
    for member in range(1, MEMBERS):
        total = total + received_ref[member].astype(f32)
    latent_grad_ref[...] = total[:HEAD]
    loss_ref[...] = jnp.broadcast_to(jnp.sum(total[HEAD : HEAD + 1, :], axis=1, keepdims=True), (8, LANES))


def call(body, outs, scratch, cost, *operands):
    specs = [
        pl.BlockSpec(memory_space=pltpu.SMEM if o.dtype == jnp.int32 and o.ndim == 1 else pltpu.VMEM)
        for o in operands
    ]
    result = pl.pallas_call(
        body,
        out_shape=tuple(jax.ShapeDtypeStruct(shape, kind) for shape, kind in outs),
        in_specs=specs,
        out_specs=tuple(pl.BlockSpec(memory_space=pltpu.VMEM) for _ in outs),
        scratch_shapes=[pltpu.VMEM(shape, kind) for shape, kind in scratch],
        compiler_params=pltpu.CompilerParams(vmem_limit_bytes=40 * 1024 * 1024),
        cost_estimate=pl.CostEstimate(flops=cost, bytes_accessed=4_000_000, transcendentals=0),
    )(*operands)
    return result


def both_ways(block):
    count = lax.axis_size(NODE)
    low = lax.ppermute(block, NODE, [(i, i + 1) for i in range(count - 1)])
    high = lax.ppermute(block, NODE, [(i + 1, i) for i in range(count - 1)])
    return low, high


def flat(y, xl, c, z, xh):
    return (((y * 2 + xl) * 2 + c) * 16 + z) * 2 + xh


def rank(y, xl, c):
    return c * 8 + y * 2 + xl


def members():
    return [(y, xl, c) for y in range(4) for xl in range(2) for c in range(2)]


def weight_route():
    by_rank = {rank(*member): member for member in members()}
    pairs = []
    for member in members():
        for z in range(16):
            for xh in range(2):
                source = flat(*by_rank[z], rank(*member), xh)
                pairs.append((source, flat(*member, z, xh)))
    return pairs


def loss_route(step):
    pairs = []
    for index, member in enumerate(members()):
        for node in range(32):
            target = (node + 2 * index + step) % 32
            pairs.append((flat(*member, node // 2, node % 2), flat(*member, target // 2, target % 2)))
    return pairs


def shards(
    latent,
    member_perturbations,
    layer_norm_gain,
    query_key_value_weight,
    output_weight_matrix,
    decoder_weight_matrix,
    observed_truth,
    region_mask,
    node_window_halfspan,
):
    pert = member_perturbations[0]
    node_total = ROWS * lax.axis_size(NODE)
    core = lax.axis_index("c")
    member = lax.axis_index(MEMBER)
    place = jnp.stack([core, lax.axis_index(NODE) * ROWS, jnp.int32(node_total)]).astype(jnp.int32)

    packed = jnp.concatenate(
        [
            query_key_value_weight,
            jnp.concatenate([output_weight_matrix[:, :INNER], output_weight_matrix[:, INNER:]], axis=0),
        ],
        axis=1,
    )
    with jax.named_scope("weights_over_node"):
        mine = lax.ppermute(packed, EVERY, weight_route())
    with jax.named_scope("latent_halo"):
        shared = jnp.concatenate(
            [latent.T, jnp.pad(node_window_halfspan.astype(bf16)[None], ((0, 15), (0, 0)))], axis=0
        )
        shared_low, shared_high = both_ways(shared)
        extended = jnp.concatenate([shared_low, shared, shared_high], axis=1)
        reach_row = extended[HEAD : HEAD + 8].astype(jnp.int32)
    with jax.named_scope("perturbation_halo"):
        pert_low, pert_high = both_ways(pert)
    with jax.named_scope("latent_over_member"):
        latent_turned = lax.all_gather(extended[:HEAD], MEMBER, axis=0, tiled=True)
    with jax.named_scope("weights_over_member"):
        wa = lax.all_to_all(
            jnp.broadcast_to(mine[None], (16,) + mine.shape), ("y", "xl", "xh"), 0, 0, tiled=True
        )
    with jax.named_scope("weights_over_core"):
        wb = lax.ppermute(wa, "c", [(0, 1), (1, 0)])

    reach_column = node_window_halfspan[:, None]
    decoder = jnp.pad(decoder_weight_matrix, ((0, LANES - VARS), (0, 0)))
    truth = lax.dynamic_slice_in_dim(observed_truth, member * SLOT, SLOT, 1)
    truth = jnp.pad(truth.T, ((0, 0), (0, LANES - VARS)))
    mask = lax.dynamic_slice_in_dim(region_mask, member * SLOT, SLOT, 0)
    area = (1.0 - (1.0 - region_share) * mask.astype(f32))[:, None]
    gain = layer_norm_gain[None]

    with jax.named_scope("layer_norm"):
        normed, latent_own = call(
            norm_kernel,
            [((EXT, WIDTH), bf16), ((ROWS, WIDTH), bf16)],
            [],
            1_000_000_000,
            latent_turned, pert_low, pert, pert_high, gain,
        )
    with jax.named_scope("forward"):
        q, k, v, unit, factor, mixed, total, forecast = call(
            forward_kernel,
            [((EXT, INNER), bf16)] * 3
            + [((ROWS, WIDTH), f32)] * 2
            + [((ROWS, INNER), f32)] * 2
            + [((ROWS, LANES), f32)],
            [((2, TILE, WINDOW), f32), ((ROWS, INNER), bf16)],
            4_000_000_000,
            place, normed, wa, wb, latent_own, pert, reach_column, decoder,
        )
    with jax.named_scope("forecasts_over_member"):
        forecasts = lax.all_to_all(
            forecast.reshape(MEMBERS, SLOT, LANES), MEMBER, 0, 0, tiled=True
        )
    with jax.named_scope("score"):
        (pred_grads,) = call(
            score_kernel, [((MEMBERS, SLOT, LANES), bf16)], [], 10_000_000, forecasts, truth, area
        )
    with jax.named_scope("gradients_over_member"):
        pred_grad = lax.all_to_all(pred_grads, MEMBER, 0, 0, tiled=True).reshape(ROWS, LANES)
    with jax.named_scope("upstream"):
        upd, scaled, g0, g1, message, loss_part = call(
            upstream_kernel,
            [((ROWS, WIDTH), f32)] + [((ROWS, INNER), bf16)] * 3 + [((ROWS, LANES), bf16), ((8, LANES), f32)],
            [((ROWS, INNER), f32)],
            500_000_000,
            place, pred_grad, decoder, wa, wb, mixed, total,
        )
    with jax.named_scope("gradient_halo"):
        message_low, message_high = both_ways(message)
    with jax.named_scope("loss_over_node"):
        loss_a = lax.ppermute(loss_part, EVERY, loss_route(0))
        loss_b = lax.ppermute(loss_part, EVERY, loss_route(1))
    with jax.named_scope("query_gradients"):
        (qgrad,) = call(
            query_kernel,
            [((ROWS, INNER), f32)],
            [((2, TILE, WINDOW), f32)],
            4_000_000_000,
            place, q, k, v, g0, g1, reach_column,
        )
    with jax.named_scope("backward"):
        noise, send = call(
            backward_kernel,
            [((ROWS, WIDTH), f32), ((MEMBERS, HEAD + 16, ROWS), bf16)],
            [((EXT, INNER), bf16)] * 3
            + [((2, TILE, WINDOW), f32), ((ROWS, INNER), f32), ((ROWS, WIDTH), f32), ((ROWS, WIDTH), f32)],
            4_000_000_000,
            place, message_low, message_high, decoder, wa, wb, q, k, v, scaled, g0, g1, reach_row,
            qgrad, unit, factor, latent_own, pert, gain, upd, loss_a, loss_b,
        )
    with jax.named_scope("latent_gradient_over_member"):
        received = lax.all_to_all(send, MEMBER, 0, 0, tiled=True)
    with jax.named_scope("finish"):
        latent_grad, loss = call(
            finish_kernel, [((HEAD, ROWS), f32), ((8, LANES), f32)], [], 10_000_000, received
        )
    loss = loss[0, 0] / (MEMBERS * node_total * VARS)
    return (loss, latent_grad.T, noise[None])


def solution(mesh):
    fine = Mesh(mesh.devices.reshape(4, 2, 2, 16, 2), EVERY)
    placed = (
        P(NODE, MEMBER),
        P(MEMBER, NODE, None),
        P(),
        P(NODE, None),
        P(NODE, None),
        P(),
        P(None, NODE),
        P(NODE),
        P(NODE),
    )
    return jax.shard_map(
        shards,
        mesh=fine,
        in_specs=placed,
        out_specs=(P(), P(NODE, MEMBER), P(MEMBER, NODE, None)),
        check_vma=False,
    )
```

```python
import functools
import math

import jax
import jax.numpy as jnp
from jax import lax
from jax.experimental import pallas as pl
from jax.experimental.pallas import tpu as pltpu
from jax.sharding import Mesh, PartitionSpec as P

HEADS = 8
HEAD = 64
INNER = 512
ROWS = 256
HALF = 256
EXT = ROWS + 2 * HALF
WIDTH = 1024
VARS = 98
LANES = 128
MEMBERS = 16
SLOT = ROWS // MEMBERS
TILE = 128
WINDOW = TILE + 2 * HALF
LOSS_LANE = 122
REACH_LANE = 125
BLOCK = 256
PACKED = 2048

norm_epsilon = 1e-05
head_epsilon = 1e-06
smooth_width = 0.1
region_share = 0.25
exponent_scale = math.log2(math.e) / 8.0

MEMBER = ("y", "xl", "c")
NODE = ("z", "xh")
EVERY = MEMBER + NODE

bf16 = jnp.bfloat16
f32 = jnp.float32


def mm(left, right):
    return lax.dot_general(left, right, (((1,), (0,)), ((), ())), preferred_element_type=f32)


def mm_t(left, right):
    return lax.dot_general(left, right, (((1,), (1,)), ((), ())), preferred_element_type=f32)


def split(value):
    high = value.astype(bf16)
    return high, (value - high.astype(f32)).astype(bf16)


def segment_matrix(scale):
    rows = lax.broadcasted_iota(jnp.int32, (BLOCK, BLOCK), 0) // HEAD
    columns = lax.broadcasted_iota(jnp.int32, (BLOCK, BLOCK), 1) // HEAD
    return jnp.where(rows == columns, scale, 0.0).astype(bf16)


def head_sums(value, segments):
    high, low = split(value)
    parts = []
    for start in range(0, INNER, BLOCK):
        lanes = slice(start, start + BLOCK)
        parts.append(mm(high[:, lanes], segments) + mm(low[:, lanes], segments))
    return jnp.concatenate(parts, axis=1)


def lane_index(rows, lanes):
    return lax.broadcasted_iota(jnp.int32, (rows, lanes), 1)


def norm_kernel(lat_ref, pert_ref, gain_ref, normed_ref, latent_ref):
    gain = gain_ref[...].astype(f32)
    for part in range(2):
        rows = slice(part * TILE, (part + 1) * TILE)
        lat = lat_ref[:, rows].astype(f32).T
        latent_ref[rows, :] = lat.astype(bf16)
        hidden = lat + pert_ref[rows, :].astype(f32)
        centred = hidden - jnp.mean(hidden, axis=1, keepdims=True)
        inverse = lax.rsqrt(jnp.mean(centred * centred, axis=1, keepdims=True) + norm_epsilon)
        normed_ref[rows, :] = (centred * inverse * gain).astype(bf16)


def out_weights(w_ref, side):
    rows = slice(side * 16, side * 16 + 16)
    return w_ref[:, rows, 3 * INNER :].reshape(INNER // 2, INNER)


def qkv_weights(w_ref, part):
    return w_ref[:, :, part * INNER : (part + 1) * INNER].reshape(INNER, INNER)


def core_halves(place_ref, size):
    core = place_ref[2]
    return (
        pl.ds(pl.multiple_of(core * size, size), size),
        pl.ds(pl.multiple_of((1 - core) * size, size), size),
    )


def column_of(row_ref):
    row = jnp.broadcast_to(row_ref[...].astype(f32), (LANES, ROWS))
    return row.T.astype(jnp.int32)


def forward_kernel(
    place_ref, low_ref, own_ref, high_ref, wa_ref, wb_ref, latent_ref, pert_ref, reach_ref, decoder_ref,
    q_ref, k_ref, v_ref, unit_ref, factor_ref, mixed_ref, total_ref, forecast_ref,
    bias_ref, mixed_low_ref,
):
    row_start = place_ref[0]
    segments = segment_matrix(1.0 / HEAD)
    near, far = core_halves(place_ref, INNER)
    for block, normed_ref in enumerate((low_ref, own_ref, high_ref)):
        rows = slice(block * ROWS, (block + 1) * ROWS)
        left, right = normed_ref[:, near], normed_ref[:, far]
        for part, out_ref in enumerate((q_ref, k_ref, v_ref)):
            projected = mm(left, qkv_weights(wa_ref, part)) + mm(right, qkv_weights(wb_ref, part))
            if part < 2:
                factor = lax.rsqrt(head_sums(projected * projected, segments) + head_epsilon)
                unit = projected * factor
                if block == 1:
                    unit_ref[:, part * INNER : (part + 1) * INNER] = unit
                    factor_ref[:, part * INNER : (part + 1) * INNER] = factor
                projected = unit
            out_ref[rows, :] = projected.astype(bf16)

    column = column_of(reach_ref)
    for tile in range(2):
        offset = (
            lane_index(TILE, WINDOW)
            - HALF
            - lax.broadcasted_iota(jnp.int32, (TILE, WINDOW), 0)
        )
        position = row_start - HALF + tile * TILE + lane_index(TILE, WINDOW)
        reach = column[tile * TILE : (tile + 1) * TILE, 0:1]
        inside = (offset >= -reach) & (offset < reach) & (position >= 0) & (position < place_ref[1])
        bias_ref[tile] = jnp.where(inside, 0.0, -1e30)

    first = lane_index(1, LANES) < HEAD

    for pair in range(HEADS // 2):
        lanes = slice(pair * LANES, (pair + 1) * LANES)
        for tile in range(2):
            rows = slice(tile * TILE, (tile + 1) * TILE)
            window = slice(tile * TILE, tile * TILE + WINDOW)
            queries = q_ref[ROWS + tile * TILE : ROWS + (tile + 1) * TILE, lanes]
            keys = k_ref[window, lanes]
            values = v_ref[window, lanes]
            bias = bias_ref[tile]
            outs = []
            for mine in (first, ~first):
                score = mm_t(jnp.where(mine, queries, jnp.zeros_like(queries)), keys)
                weight = jnp.exp2(score * exponent_scale + bias).astype(bf16)
                outs.append(mm(weight, jnp.where(mine, values, jnp.ones_like(values))))
            total = pltpu.roll(jnp.where(first, outs[1], outs[0]), HEAD, 1)
            mixed = jnp.where(first, outs[0], outs[1]) / total
            mixed_ref[rows, lanes] = mixed
            mixed_low_ref[rows, lanes] = mixed.astype(bf16)
            total_ref[rows, lanes] = total

    near, far = core_halves(place_ref, INNER // 2)
    left, right = mixed_low_ref[:, near], mixed_low_ref[:, far]
    forecast = jnp.zeros((ROWS, LANES), f32)
    for side in range(2):
        columns = slice(side * INNER, (side + 1) * INNER)
        branch = mm(left, out_weights(wa_ref, side)) + mm(right, out_weights(wb_ref, side))
        hidden = latent_ref[:, columns].astype(f32) + pert_ref[:, columns].astype(f32)
        updated = (hidden + branch).astype(bf16)
        forecast = forecast + mm_t(updated, decoder_ref[:, columns])
    forecast_ref[...] = forecast


def score_kernel(forecast_ref, truth_ref, area_ref, out_ref):
    lanes = lane_index(SLOT, LANES)
    area = jnp.where(lanes < VARS, area_ref[...], 0.0)
    truth = truth_ref[...]
    square = smooth_width * smooth_width
    loss = jnp.zeros((SLOT, LANES), f32)
    for member in range(MEMBERS):
        own = forecast_ref[member]
        pull = jnp.zeros((SLOT, LANES), f32)
        spread = jnp.zeros((SLOT, LANES), f32)
        for other in range(MEMBERS):
            if other == member:
                continue
            gap = own - forecast_ref[other]
            power = gap * gap + square
            inverse = lax.rsqrt(power)
            pull = pull + gap * inverse
            spread = spread + power * inverse
        gap = own - truth
        power = gap * gap + square
        inverse = lax.rsqrt(power)
        loss = loss + area * (power * inverse - spread * (0.5 / (MEMBERS - 1)))
        out_ref[member] = (area * (gap * inverse - pull * (1.0 / (MEMBERS - 1)))).astype(bf16)
    total = jnp.sum(jnp.sum(loss, axis=1, keepdims=True), axis=0, keepdims=True)
    total = jnp.broadcast_to(total, (SLOT, LANES))
    high, rest = split(total)
    middle = rest
    low = (total - high.astype(f32) - middle.astype(f32)).astype(bf16)
    for member in range(MEMBERS):
        kept = out_ref[member]
        kept = jnp.where(lanes == VARS, high, kept)
        kept = jnp.where(lanes == VARS + 1, middle, kept)
        out_ref[member] = jnp.where(lanes == VARS + 2, low, kept)


def mixed_gradient(upd_low, place_ref, wa_ref, wb_ref, target_ref):
    for w_ref, lanes in zip((wa_ref, wb_ref), core_halves(place_ref, INNER // 2)):
        target_ref[:, lanes] = mm_t(upd_low[:, :INNER], out_weights(w_ref, 0)) + mm_t(
            upd_low[:, INNER:], out_weights(w_ref, 1)
        )
    return target_ref[...].astype(bf16).astype(f32)


def gradient_operands(scaled, row_dot, g0_ref, g1_ref, rows):
    first = lane_index(1, LANES) < HEAD
    spot = lane_index(ROWS, LANES) % HEAD
    for pair in range(HEADS // 2):
        lanes = slice(pair * LANES, (pair + 1) * LANES)
        high, low = split(-pltpu.roll(row_dot[:, lanes], HEAD, 1))
        zero = jnp.zeros_like(high)
        extra = jnp.where(spot == 0, high, jnp.where(spot == 1, low, zero))
        own = scaled[:, lanes]
        g0_ref[rows, lanes] = jnp.where(first, own, extra)
        g1_ref[rows, lanes] = jnp.where(first, extra, own)


def pick(rows, lanes):
    row = lax.broadcasted_iota(jnp.int32, (rows, lanes), 0)
    lane = lane_index(rows, lanes)
    return row, lane


def upstream_kernel(
    place_ref, pg_ref, decoder_ref, wa_ref, wb_ref, mixed_ref, total_ref, reach_ref,
    upd_ref, scaled_ref, g0_ref, g1_ref, message_ref, loss_ref, grad_ref,
):
    pg = pg_ref[...]
    upd = mm(pg, decoder_ref[...])
    upd_ref[...] = upd
    everything = slice(0, ROWS)
    grad = mixed_gradient(upd.astype(bf16), place_ref, wa_ref, wb_ref, grad_ref)
    total = total_ref[...]
    inverse = 1.0 / total
    row_dot = head_sums(grad * mixed_ref[...], segment_matrix(1.0)) * inverse
    scaled = (grad * inverse).astype(bf16)
    scaled_ref[...] = scaled
    gradient_operands(scaled, row_dot, g0_ref, g1_ref, everything)

    row, lane = pick(INNER, LANES)
    head_row = (row % HEAD == 0)
    chosen = lambda start: jnp.where(head_row & (lane == start + row // HEAD), 1.0, 0.0).astype(bf16)
    high, low = split(total)
    stats = mm(high, chosen(VARS)) + mm(low, chosen(VARS + 8)) + mm(row_dot.astype(bf16), chosen(VARS + 16))
    lanes = lane_index(ROWS, LANES)
    message = jnp.where(lanes < VARS, pg.astype(f32), stats)
    message = jnp.where(lanes == REACH_LANE, column_of(reach_ref).astype(f32), message)
    kept = jnp.where((lanes >= VARS) & (lanes < VARS + 3), pg.astype(f32), 0.0)
    loss = jnp.sum(jnp.sum(kept, axis=1, keepdims=True), axis=0, keepdims=True) * (1.0 / SLOT)
    loss_ref[...] = jnp.broadcast_to(loss, (8, LANES))
    high, middle = split(loss)
    low = (loss - high.astype(f32) - middle.astype(f32)).astype(bf16)
    for lane, part in enumerate((high, middle, low)):
        message = jnp.where(lanes == LOSS_LANE + lane, part.astype(f32), message)
    message_ref[...] = message.astype(bf16)


def pair_kernel(place_ref, own_ref, low_ref, high_ref, out_ref):
    lanes = lane_index(1, LANES)
    even = place_ref[3] == 0
    nearby = jnp.where(even, high_ref[0:16, :].astype(f32), low_ref[0:16, :].astype(f32))[0:1, :]
    nearby = jnp.where((lanes >= LOSS_LANE) & (lanes < LOSS_LANE + 3), nearby, 0.0)
    out_ref[...] = own_ref[...] + jnp.sum(nearby, axis=1, keepdims=True)


def query_kernel(
    place_ref, q_ref, k_ref, v_ref, g0_ref, g1_ref, reach_ref, qgrad_ref, bias_ref,
):
    row_start = place_ref[0]
    column = column_of(reach_ref)
    for tile in range(2):
        offset = (
            lane_index(TILE, WINDOW)
            - HALF
            - lax.broadcasted_iota(jnp.int32, (TILE, WINDOW), 0)
        )
        position = row_start - HALF + tile * TILE + lane_index(TILE, WINDOW)
        reach = column[tile * TILE : (tile + 1) * TILE, 0:1]
        inside = (offset >= -reach) & (offset < reach) & (position >= 0) & (position < place_ref[1])
        bias_ref[tile] = jnp.where(inside, 0.0, -1e30)
    first = lane_index(1, LANES) < HEAD

    for pair in range(HEADS // 2):
        lanes = slice(pair * LANES, (pair + 1) * LANES)
        for tile in range(2):
            rows = slice(tile * TILE, (tile + 1) * TILE)
            window = slice(tile * TILE, tile * TILE + WINDOW)
            queries = q_ref[ROWS + tile * TILE : ROWS + (tile + 1) * TILE, lanes]
            keys = k_ref[window, lanes]
            values = v_ref[window, lanes]
            bias = bias_ref[tile]
            grads = []
            for mine, g_ref in ((first, g0_ref), (~first, g1_ref)):
                score = mm_t(jnp.where(mine, queries, jnp.zeros_like(queries)), keys)
                weight = jnp.exp2(score * exponent_scale + bias)
                pull = mm_t(g_ref[rows, lanes], jnp.where(mine, values, jnp.ones_like(values)))
                grads.append(mm((weight * pull).astype(bf16), keys))
            qgrad_ref[rows, lanes] = jnp.where(first, grads[0], grads[1]) * 0.125


def backward_kernel(
    place_ref, low_ref, high_ref, decoder_ref, wa_ref, wb_ref, q_ref, k_ref, v_ref,
    scaled_ref, g0_ref, g1_ref, reach_ref, qgrad_ref, unit_ref, factor_ref,
    qkv_grad_ref,
    all_scaled, all_g0, all_g1, all_reach, bias_ref, grad_ref, kv_ref,
):
    row, lane = pick(LANES, INNER)
    spread = lambda start: row == start + lane // HEAD
    expand_total = jnp.where(spread(VARS) | spread(VARS + 8), 1.0, 0.0).astype(bf16)
    expand_dot = jnp.where(spread(VARS + 16), 1.0, 0.0).astype(bf16)
    middle = slice(ROWS, 2 * ROWS)
    all_scaled[middle, :] = scaled_ref[...]
    all_g0[middle, :] = g0_ref[...]
    all_g1[middle, :] = g1_ref[...]
    all_reach[:, middle] = jnp.broadcast_to(reach_ref[...], (8, ROWS))
    for block, message_ref in ((0, low_ref), (2, high_ref)):
        rows = slice(block * ROWS, (block + 1) * ROWS)
        message = message_ref[...]
        turned = message.astype(f32).T
        all_reach[:, rows] = jnp.broadcast_to(turned[REACH_LANE : REACH_LANE + 1, :], (8, ROWS)).astype(jnp.int32)
        grad = mixed_gradient(
            mm(message, decoder_ref[...]).astype(bf16), place_ref, wa_ref, wb_ref, grad_ref
        )
        total = mm(message, expand_total)
        scaled = (grad / jnp.where(total > 0.0, total, 1.0)).astype(bf16)
        all_scaled[rows, :] = scaled
        gradient_operands(scaled, mm(message, expand_dot), all_g0, all_g1, rows)

    for tile in range(2):
        offset = (
            HALF
            + lax.broadcasted_iota(jnp.int32, (TILE, WINDOW), 0)
            - lane_index(TILE, WINDOW)
        )
        reach = all_reach[0:1, tile * TILE : tile * TILE + WINDOW]
        bias_ref[tile] = jnp.where((offset >= -reach) & (offset < reach), 0.0, -1e30)
    first = lane_index(1, LANES) < HEAD

    for pair in range(HEADS // 2):
        lanes = slice(pair * LANES, (pair + 1) * LANES)
        value_lanes = slice(INNER + pair * LANES, INNER + (pair + 1) * LANES)
        for tile in range(2):
            rows = slice(tile * TILE, (tile + 1) * TILE)
            window = slice(tile * TILE, tile * TILE + WINDOW)
            keys = k_ref[ROWS + tile * TILE : ROWS + (tile + 1) * TILE, lanes]
            values = v_ref[ROWS + tile * TILE : ROWS + (tile + 1) * TILE, lanes]
            queries = q_ref[window, lanes]
            scaled = all_scaled[window, lanes]
            bias = bias_ref[tile]
            key_grads = []
            value_grads = []
            for mine, g_ref in ((first, all_g0), (~first, all_g1)):
                score = mm_t(jnp.where(mine, keys, jnp.zeros_like(keys)), queries)
                weight = jnp.exp2(score * exponent_scale + bias)
                pull = mm_t(jnp.where(mine, values, jnp.ones_like(values)), g_ref[window, lanes])
                value_grads.append(mm(weight.astype(bf16), scaled))
                key_grads.append(mm((weight * pull).astype(bf16), queries))
            kv_ref[rows, lanes] = jnp.where(first, key_grads[0], key_grads[1]) * 0.125
            kv_ref[rows, value_lanes] = jnp.where(first, value_grads[0], value_grads[1])

    segments = segment_matrix(1.0 / HEAD)
    for part, grad in ((0, qgrad_ref[...]), (1, kv_ref[:, :INNER])):
        columns = slice(part * INNER, (part + 1) * INNER)
        unit = unit_ref[:, columns]
        along = head_sums(grad * unit, segments)
        qkv_grad_ref[:, columns] = (factor_ref[:, columns] * (grad - unit * along)).astype(bf16)
    qkv_grad_ref[:, 2 * INNER :] = kv_ref[:, INNER:].astype(bf16)


def hidden_kernel(
    place_ref, qkv_grad_ref, wa_ref, wb_ref, latent_ref, pert_ref, gain_ref, upd_ref, loss_ref,
    noise_ref, send_ref, normed_grad_ref,
):
    parts = [qkv_grad_ref[:, part * INNER : (part + 1) * INNER] for part in range(3)]
    for w_ref, lanes in zip((wa_ref, wb_ref), core_halves(place_ref, INNER)):
        normed_grad_ref[:, lanes] = (
            mm_t(parts[0], qkv_weights(w_ref, 0))
            + mm_t(parts[1], qkv_weights(w_ref, 1))
            + mm_t(parts[2], qkv_weights(w_ref, 2))
        )
    gain = gain_ref[...].astype(f32)
    for part in range(2):
        rows = slice(part * TILE, (part + 1) * TILE)
        hidden = latent_ref[rows, :].astype(f32) + pert_ref[rows, :].astype(f32)
        centred = hidden - jnp.mean(hidden, axis=1, keepdims=True)
        inverse = lax.rsqrt(jnp.mean(centred * centred, axis=1, keepdims=True) + norm_epsilon)
        standard = centred * inverse
        grad = normed_grad_ref[rows, :] * gain
        first_term = jnp.mean(grad, axis=1, keepdims=True)
        second_term = standard * jnp.mean(grad * standard, axis=1, keepdims=True)
        result = upd_ref[rows, :] + inverse * (grad - first_term - second_term)
        noise_ref[rows, :] = result
        turned = result.T.astype(bf16)
        for member in range(MEMBERS):
            send_ref[member, :HEAD, rows] = turned[member * HEAD : (member + 1) * HEAD, :]
    loss = jnp.broadcast_to(loss_ref[0:1, 0:1], (16, ROWS))
    high, middle = split(loss)
    low = (loss - high.astype(f32) - middle.astype(f32)).astype(bf16)
    lanes = lane_index(16, ROWS)
    tail = jnp.zeros((16, ROWS), f32)
    for lane, part in enumerate((high, middle, low)):
        tail = jnp.where(lanes == lane, part.astype(f32), tail)
    for member in range(MEMBERS):
        send_ref[member, HEAD:, :] = tail.astype(bf16)


def finish_kernel(received_ref, latent_grad_ref, loss_ref):
    total = received_ref[0].astype(f32)
    for member in range(1, MEMBERS):
        total = total + received_ref[member].astype(f32)
    latent_grad_ref[...] = total[:HEAD]
    loss_ref[...] = jnp.broadcast_to(jnp.sum(total[HEAD : HEAD + 1, :], axis=1, keepdims=True), (8, LANES))


def call(body, outs, scratch, megabytes, cost, *operands, far=()):
    spaces = [
        pltpu.SMEM if o.dtype == jnp.int32 and o.ndim == 1 else pltpu.HBM if i in far else pltpu.VMEM
        for i, o in enumerate(operands)
    ]
    specs = [pl.BlockSpec(memory_space=space) for space in spaces]
    semaphores = [pltpu.SemaphoreType.DMA((len(far),))] if far else []
    result = pl.pallas_call(
        body,
        out_shape=tuple(jax.ShapeDtypeStruct(shape, kind) for shape, kind in outs),
        in_specs=specs,
        out_specs=tuple(pl.BlockSpec(memory_space=pltpu.VMEM) for _ in outs),
        scratch_shapes=[pltpu.VMEM(shape, kind) for shape, kind in scratch] + semaphores,
        compiler_params=pltpu.CompilerParams(vmem_limit_bytes=megabytes * 1024 * 1024),
        cost_estimate=pl.CostEstimate(flops=cost, bytes_accessed=4_000_000, transcendentals=0),
    )(*operands)
    return result


def both_ways(block):
    count = lax.axis_size(NODE)
    low = lax.ppermute(block, NODE, [(i, i + 1) for i in range(count - 1)])
    high = lax.ppermute(block, NODE, [(i + 1, i) for i in range(count - 1)])
    return low, high


def flat(y, xl, c, z, xh):
    return (((y * 2 + xl) * 2 + c) * 16 + z) * 2 + xh


def rank(y, xl, c):
    return c * 8 + y * 2 + xl


def members():
    return [(y, xl, c) for y in range(4) for xl in range(2) for c in range(2)]


def weight_route():
    by_rank = {rank(*member): member for member in members()}
    pairs = []
    for member in members():
        for z in range(16):
            for xh in range(2):
                source = flat(*by_rank[z], rank(*member), xh)
                pairs.append((source, flat(*member, z, xh)))
    return pairs


def loss_route():
    pairs = []
    for shift, member in enumerate(members()):
        for z in range(16):
            for xh in range(2):
                pairs.append((flat(*member, z, xh), flat(*member, (z + shift) % 16, xh)))
    return pairs


def shards(
    latent,
    member_perturbations,
    layer_norm_gain,
    query_key_value_weight,
    output_weight_matrix,
    decoder_weight_matrix,
    observed_truth,
    region_mask,
    node_window_halfspan,
):
    pert = member_perturbations[0]
    node_total = ROWS * lax.axis_size(NODE)
    member = lax.axis_index(MEMBER)
    place = jnp.stack([lax.axis_index(NODE) * ROWS, jnp.int32(node_total), lax.axis_index("c"), lax.axis_index("xh")]).astype(jnp.int32)

    packed = jnp.concatenate(
        [
            query_key_value_weight,
            jnp.concatenate([output_weight_matrix[:, :INNER], output_weight_matrix[:, INNER:]], axis=0),
        ],
        axis=1,
    )
    with jax.named_scope("weights_over_node"):
        mine = lax.ppermute(packed, EVERY, weight_route())
    decoder = jnp.pad(decoder_weight_matrix, ((0, LANES - VARS), (0, 0)))
    truth = lax.dynamic_slice_in_dim(observed_truth, member * SLOT, SLOT, 1)
    truth = jnp.pad(truth.T, ((0, 0), (0, LANES - VARS)))
    mask = lax.dynamic_slice_in_dim(region_mask, member * SLOT, SLOT, 0)
    area = (1.0 - (1.0 - region_share) * mask.astype(f32))[:, None]
    area = jnp.broadcast_to(area, (SLOT, LANES))
    latent_copies = jnp.broadcast_to(latent.T[None], (MEMBERS, HEAD, ROWS))
    place, reach_row, decoder, truth, area, gain, latent_copies = lax.optimization_barrier(
        (place, node_window_halfspan[None], decoder, truth, area,
         layer_norm_gain[None], latent_copies)
    )
    with jax.named_scope("latent_over_member"):
        latent_turned = lax.all_to_all(latent_copies, MEMBER, 0, 0, tiled=True).reshape(WIDTH, ROWS)
    with jax.named_scope("layer_norm"):
        normed, latent_own = call(
            norm_kernel,
            [((ROWS, WIDTH), bf16), ((ROWS, WIDTH), bf16)],
            [],
            8,
            1_000_000_000,
            latent_turned, pert, gain,
        )
    mine, normed = lax.optimization_barrier((mine, normed))
    with jax.named_scope("normed_halo"):
        normed_low, normed_high = both_ways(normed)
    with jax.named_scope("weights_over_x"):
        row = lax.all_to_all(jnp.broadcast_to(mine[None], (4,) + mine.shape), ("xl", "xh"), 0, 0, tiled=True)
        row = row.reshape(128, PACKED)
    with jax.named_scope("weights_over_y"):
        wa = lax.all_to_all(jnp.broadcast_to(row[None], (4,) + row.shape), "y", 0, 0, tiled=True)
        wa = wa.reshape(16, 32, PACKED)
    wa, normed_low, normed_high = lax.optimization_barrier((wa, normed_low, normed_high))
    with jax.named_scope("weights_over_core"):
        wb = lax.ppermute(wa, "c", [(0, 1), (1, 0)])
    with jax.named_scope("forward"):
        q, k, v, unit, factor, mixed, total, forecast = call(
            forward_kernel,
            [((EXT, INNER), bf16)] * 3
            + [((ROWS, WIDTH), f32)] * 2
            + [((ROWS, INNER), f32)] * 2
            + [((ROWS, LANES), f32)],
            [((2, TILE, WINDOW), f32), ((ROWS, INNER), bf16)],
            40,
            4_000_000_000,
            place, normed_low, normed, normed_high, wa, wb, latent_own, pert, reach_row, decoder,
        )
    with jax.named_scope("forecasts_over_member"):
        forecasts = lax.all_to_all(
            forecast.reshape(MEMBERS, SLOT, LANES), MEMBER, 0, 0, tiled=True
        )
    with jax.named_scope("score"):
        (pred_grads,) = call(
            score_kernel, [((MEMBERS, SLOT, LANES), bf16)], [], 8, 10_000_000, forecasts, truth, area
        )
    with jax.named_scope("gradients_over_member"):
        pred_grad = lax.all_to_all(pred_grads, MEMBER, 0, 0, tiled=True).reshape(ROWS, LANES)
    with jax.named_scope("upstream"):
        upd, scaled, g0, g1, message, loss_part = call(
            upstream_kernel,
            [((ROWS, WIDTH), f32)] + [((ROWS, INNER), bf16)] * 3 + [((ROWS, LANES), bf16), ((8, LANES), f32)],
            [((ROWS, INNER), f32)],
            16,
            500_000_000,
            place, pred_grad, decoder, wa, wb, mixed, total, reach_row,
        )
    with jax.named_scope("gradient_halo"):
        message_low, message_high = both_ways(message)
    with jax.named_scope("query_gradients"):
        (qgrad,) = call(
            query_kernel,
            [((ROWS, INNER), f32)],
            [((2, TILE, WINDOW), f32)],
            12,
            4_000_000_000,
            place, q, k, v, g0, g1, reach_row,
        )
    with jax.named_scope("loss_over_node"):
        (loss_part,) = call(
            pair_kernel, [((8, LANES), f32)], [], 4, 10_000, place, loss_part, message_low, message_high
        )
        loss_part = lax.ppermute(loss_part, EVERY, loss_route())
    with jax.named_scope("backward"):
        (qkv_grad,) = call(
            backward_kernel,
            [((ROWS, 3 * INNER), bf16)],
            [((EXT, INNER), bf16)] * 3
            + [((8, EXT), jnp.int32)]
            + [((2, TILE, WINDOW), f32), ((ROWS, INNER), f32), ((ROWS, WIDTH), f32)],
            24,
            4_000_000_000,
            place, message_low, message_high, decoder, wa, wb, q, k, v, scaled, g0, g1, reach_row,
            qgrad, unit, factor,
        )
    with jax.named_scope("hidden_gradient"):
        noise, send = call(
            hidden_kernel,
            [((ROWS, WIDTH), f32), ((MEMBERS, HEAD + 16, ROWS), bf16)],
            [((ROWS, WIDTH), f32)],
            16,
            1_000_000_000,
            place, qkv_grad, wa, wb, latent_own, pert, gain, upd, loss_part,
        )
    with jax.named_scope("latent_gradient_over_member"):
        received = lax.all_to_all(send, MEMBER, 0, 0, tiled=True)
    with jax.named_scope("finish"):
        latent_grad, loss = call(
            finish_kernel, [((HEAD, ROWS), f32), ((8, LANES), f32)], [], 8, 10_000_000, received
        )
    loss = loss[0, 0] / (MEMBERS * node_total * VARS)
    return (loss, latent_grad.T, noise[None])


def solution(mesh):
    fine = Mesh(mesh.devices.reshape(4, 2, 2, 16, 2), EVERY)
    placed = (
        P(NODE, MEMBER),
        P(MEMBER, NODE, None),
        P(),
        P(NODE, None),
        P(NODE, None),
        P(),
        P(None, NODE),
        P(NODE),
        P(NODE),
    )
    return jax.shard_map(
        shards,
        mesh=fine,
        in_specs=placed,
        out_specs=(P(), P(NODE, MEMBER), P(MEMBER, NODE, None)),
        check_vma=False,
    )
```

```python
import functools
import math

import jax
import jax.numpy as jnp
from jax import lax
from jax.experimental import pallas as pl
from jax.experimental.pallas import tpu as pltpu
from jax.sharding import Mesh, PartitionSpec as P

HEADS = 8
HEAD = 64
INNER = 512
ROWS = 256
HALF = 256
EXT = ROWS + 2 * HALF
WIDTH = 1024
VARS = 98
LANES = 128
MEMBERS = 16
SLOT = ROWS // MEMBERS
TILE = 256
WINDOW = TILE + 2 * HALF
LOSS_LANE = 122
REACH_LANE = 125
BLOCK = 256
PACKED = 2048

norm_epsilon = 1e-05
head_epsilon = 1e-06
smooth_width = 0.1
region_share = 0.25
exponent_scale = math.log2(math.e) / 8.0

MEMBER = ("y", "xl", "c")
NODE = ("z", "xh")
EVERY = MEMBER + NODE

bf16 = jnp.bfloat16
f32 = jnp.float32


def mm(left, right):
    return lax.dot_general(left, right, (((1,), (0,)), ((), ())), preferred_element_type=f32)


def mm_t(left, right):
    return lax.dot_general(left, right, (((1,), (1,)), ((), ())), preferred_element_type=f32)


def split(value):
    high = value.astype(bf16)
    return high, (value - high.astype(f32)).astype(bf16)


def segment_matrix(scale):
    rows = lax.broadcasted_iota(jnp.int32, (BLOCK, BLOCK), 0) // HEAD
    columns = lax.broadcasted_iota(jnp.int32, (BLOCK, BLOCK), 1) // HEAD
    return jnp.where(rows == columns, scale, 0.0).astype(bf16)


def head_sums(value, segments):
    high, low = split(value)
    parts = []
    for start in range(0, INNER, BLOCK):
        lanes = slice(start, start + BLOCK)
        parts.append(mm(high[:, lanes], segments) + mm(low[:, lanes], segments))
    return jnp.concatenate(parts, axis=1)


def head_means(value, segments):
    rounded = value.astype(bf16)
    return jnp.concatenate(
        [mm(rounded[:, start : start + BLOCK], segments) for start in range(0, INNER, BLOCK)], axis=1
    )


def lane_index(rows, lanes):
    return lax.broadcasted_iota(jnp.int32, (rows, lanes), 1)


def norm_kernel(lat_ref, pert_ref, gain_ref, normed_ref, latent_ref):
    gain = gain_ref[...].astype(f32)
    for part in range(ROWS // TILE):
        rows = slice(part * TILE, (part + 1) * TILE)
        lat = lat_ref[:, rows].astype(f32).T
        latent_ref[rows, :] = lat.astype(bf16)
        hidden = lat + pert_ref[rows, :].astype(f32)
        centred = hidden - jnp.mean(hidden, axis=1, keepdims=True)
        inverse = lax.rsqrt(jnp.mean(centred * centred, axis=1, keepdims=True) + norm_epsilon)
        normed_ref[rows, :] = (centred * inverse * gain).astype(bf16)


def out_weights(w_ref, side):
    rows = slice(side * 16, side * 16 + 16)
    return w_ref[:, rows, 3 * INNER :].reshape(INNER // 2, INNER)


def qkv_weights(w_ref, part):
    return w_ref[:, :, part * INNER : (part + 1) * INNER].reshape(INNER, INNER)


def core_halves(place_ref, size):
    core = place_ref[2]
    return (
        pl.ds(pl.multiple_of(core * size, size), size),
        pl.ds(pl.multiple_of((1 - core) * size, size), size),
    )


def column_of(row_ref):
    row = jnp.broadcast_to(row_ref[...].astype(f32), (LANES, ROWS))
    return row.T.astype(jnp.int32)


def forward_kernel(
    place_ref, normed_ref, wa_ref, wb_ref, latent_ref, pert_ref, reach_ref, decoder_ref,
    q_ref, k_ref, v_ref, unit_ref, factor_ref, mixed_ref, total_ref, forecast_ref,
    bias_ref, mixed_low_ref,
):
    row_start = place_ref[0]
    segments = segment_matrix(1.0 / HEAD)
    near, far = core_halves(place_ref, INNER)
    for block in range(3):
        rows = slice(block * ROWS, (block + 1) * ROWS)
        left, right = normed_ref[rows, near], normed_ref[rows, far]
        together = mm(left, wa_ref[:, :, : 3 * INNER].reshape(INNER, 3 * INNER)) + mm(
            right, wb_ref[:, :, : 3 * INNER].reshape(INNER, 3 * INNER)
        )
        for part, out_ref in enumerate((q_ref, k_ref, v_ref)):
            projected = together[:, part * INNER : (part + 1) * INNER]
            if part < 2:
                factor = lax.rsqrt(head_means(projected * projected, segments) + head_epsilon)
                unit = projected * factor
                if block == 1:
                    unit_ref[:, part * INNER : (part + 1) * INNER] = unit
                    factor_ref[:, part * INNER : (part + 1) * INNER] = factor
                projected = unit
            out_ref[rows, :] = projected.astype(bf16)

    column = column_of(reach_ref)
    for tile in range(ROWS // TILE):
        offset = (
            lane_index(TILE, WINDOW)
            - HALF
            - lax.broadcasted_iota(jnp.int32, (TILE, WINDOW), 0)
        )
        position = row_start - HALF + tile * TILE + lane_index(TILE, WINDOW)
        reach = column[tile * TILE : (tile + 1) * TILE, 0:1]
        inside = (offset >= -reach) & (offset < reach) & (position >= 0) & (position < place_ref[1])
        bias_ref[tile] = jnp.where(inside, 0.0, -1e30)

    first = lane_index(1, LANES) < HEAD

    for pair in range(HEADS // 2):
        lanes = slice(pair * LANES, (pair + 1) * LANES)
        for tile in range(ROWS // TILE):
            rows = slice(tile * TILE, (tile + 1) * TILE)
            window = slice(tile * TILE, tile * TILE + WINDOW)
            queries = q_ref[ROWS + tile * TILE : ROWS + (tile + 1) * TILE, lanes]
            keys = k_ref[window, lanes]
            values = v_ref[window, lanes]
            bias = bias_ref[tile]
            outs = []
            for mine in (first, ~first):
                score = mm_t(jnp.where(mine, queries, jnp.zeros_like(queries)), keys)
                weight = jnp.exp2(score * exponent_scale + bias).astype(bf16)
                outs.append(mm(weight, jnp.where(mine, values, jnp.ones_like(values))))
            total = pltpu.roll(jnp.where(first, outs[1], outs[0]), HEAD, 1)
            mixed = jnp.where(first, outs[0], outs[1]) / total
            mixed_ref[rows, lanes] = mixed
            mixed_low_ref[rows, lanes] = mixed.astype(bf16)
            total_ref[rows, lanes] = total

    near, far = core_halves(place_ref, INNER // 2)
    left, right = mixed_low_ref[:, near], mixed_low_ref[:, far]
    forecast = jnp.zeros((ROWS, LANES), f32)
    for side in range(2):
        columns = slice(side * INNER, (side + 1) * INNER)
        branch = mm(left, out_weights(wa_ref, side)) + mm(right, out_weights(wb_ref, side))
        hidden = latent_ref[:, columns].astype(f32) + pert_ref[:, columns].astype(f32)
        updated = (hidden + branch).astype(bf16)
        forecast = forecast + mm_t(updated, decoder_ref[:, columns])
    forecast_ref[...] = forecast


def score_kernel(forecast_ref, truth_ref, area_ref, out_ref):
    lanes = lane_index(SLOT, LANES)
    area = jnp.where(lanes < VARS, area_ref[...], 0.0)
    truth = truth_ref[...]
    square = smooth_width * smooth_width
    loss = jnp.zeros((SLOT, LANES), f32)
    for member in range(MEMBERS):
        own = forecast_ref[member]
        pull = jnp.zeros((SLOT, LANES), f32)
        spread = jnp.zeros((SLOT, LANES), f32)
        for other in range(MEMBERS):
            if other == member:
                continue
            gap = own - forecast_ref[other]
            power = gap * gap + square
            inverse = lax.rsqrt(power)
            pull = pull + gap * inverse
            spread = spread + power * inverse
        gap = own - truth
        power = gap * gap + square
        inverse = lax.rsqrt(power)
        loss = loss + area * (power * inverse - spread * (0.5 / (MEMBERS - 1)))
        out_ref[member] = (area * (gap * inverse - pull * (1.0 / (MEMBERS - 1)))).astype(bf16)
    total = jnp.sum(jnp.sum(loss, axis=1, keepdims=True), axis=0, keepdims=True)
    total = jnp.broadcast_to(total, (SLOT, LANES))
    high, rest = split(total)
    middle = rest
    low = (total - high.astype(f32) - middle.astype(f32)).astype(bf16)
    for member in range(MEMBERS):
        kept = out_ref[member]
        kept = jnp.where(lanes == VARS, high, kept)
        kept = jnp.where(lanes == VARS + 1, middle, kept)
        out_ref[member] = jnp.where(lanes == VARS + 2, low, kept)


def mixed_gradient(upd_low, place_ref, wa_ref, wb_ref, target_ref):
    for w_ref, lanes in zip((wa_ref, wb_ref), core_halves(place_ref, INNER // 2)):
        target_ref[:, lanes] = mm_t(upd_low[:, :INNER], out_weights(w_ref, 0)) + mm_t(
            upd_low[:, INNER:], out_weights(w_ref, 1)
        )
    return target_ref[...].astype(bf16).astype(f32)


def gradient_operands(scaled, row_dot, g0_ref, g1_ref, rows):
    first = lane_index(1, LANES) < HEAD
    spot = lane_index(ROWS, LANES) % HEAD
    for pair in range(HEADS // 2):
        lanes = slice(pair * LANES, (pair + 1) * LANES)
        high, low = split(-pltpu.roll(row_dot[:, lanes], HEAD, 1))
        zero = jnp.zeros_like(high)
        extra = jnp.where(spot == 0, high, jnp.where(spot == 1, low, zero))
        own = scaled[:, lanes]
        g0_ref[rows, lanes] = jnp.where(first, own, extra)
        g1_ref[rows, lanes] = jnp.where(first, extra, own)


def pick(rows, lanes):
    row = lax.broadcasted_iota(jnp.int32, (rows, lanes), 0)
    lane = lane_index(rows, lanes)
    return row, lane


def upstream_kernel(
    place_ref, pg_ref, decoder_ref, wa_ref, wb_ref, mixed_ref, total_ref, reach_ref,
    upd_ref, scaled_ref, g0_ref, g1_ref, message_ref, loss_ref, grad_ref,
):
    pg = pg_ref[...]
    upd = mm(pg, decoder_ref[...])
    upd_ref[...] = upd
    everything = slice(0, ROWS)
    grad = mixed_gradient(upd.astype(bf16), place_ref, wa_ref, wb_ref, grad_ref)
    total = total_ref[...]
    inverse = 1.0 / total
    row_dot = head_sums(grad * mixed_ref[...], segment_matrix(1.0)) * inverse
    scaled = (grad * inverse).astype(bf16)
    scaled_ref[...] = scaled
    gradient_operands(scaled, row_dot, g0_ref, g1_ref, everything)

    row, lane = pick(INNER, LANES)
    head_row = (row % HEAD == 0)
    chosen = lambda start: jnp.where(head_row & (lane == start + row // HEAD), 1.0, 0.0).astype(bf16)
    high, low = split(total)
    stats = mm(high, chosen(VARS)) + mm(low, chosen(VARS + 8)) + mm(row_dot.astype(bf16), chosen(VARS + 16))
    lanes = lane_index(ROWS, LANES)
    message = jnp.where(lanes < VARS, pg.astype(f32), stats)
    message = jnp.where(lanes == REACH_LANE, column_of(reach_ref).astype(f32), message)
    kept = jnp.where((lanes >= VARS) & (lanes < VARS + 3), pg.astype(f32), 0.0)
    loss = jnp.sum(jnp.sum(kept, axis=1, keepdims=True), axis=0, keepdims=True) * (1.0 / SLOT)
    loss_ref[...] = jnp.broadcast_to(loss, (8, LANES))
    high, middle = split(loss)
    low = (loss - high.astype(f32) - middle.astype(f32)).astype(bf16)
    for lane, part in enumerate((high, middle, low)):
        message = jnp.where(lanes == LOSS_LANE + lane, part.astype(f32), message)
    message_ref[...] = message.astype(bf16)


def pair_kernel(place_ref, own_ref, low_ref, high_ref, out_ref):
    lanes = lane_index(1, LANES)
    even = place_ref[3] == 0
    nearby = jnp.where(even, high_ref[0:16, :].astype(f32), low_ref[0:16, :].astype(f32))[0:1, :]
    nearby = jnp.where((lanes >= LOSS_LANE) & (lanes < LOSS_LANE + 3), nearby, 0.0)
    out_ref[...] = own_ref[...] + jnp.sum(nearby, axis=1, keepdims=True)


def query_kernel(
    place_ref, q_ref, k_ref, v_ref, g0_ref, g1_ref, reach_ref, qgrad_ref, bias_ref,
):
    row_start = place_ref[0]
    column = column_of(reach_ref)
    for tile in range(ROWS // TILE):
        offset = (
            lane_index(TILE, WINDOW)
            - HALF
            - lax.broadcasted_iota(jnp.int32, (TILE, WINDOW), 0)
        )
        position = row_start - HALF + tile * TILE + lane_index(TILE, WINDOW)
        reach = column[tile * TILE : (tile + 1) * TILE, 0:1]
        inside = (offset >= -reach) & (offset < reach) & (position >= 0) & (position < place_ref[1])
        bias_ref[tile] = jnp.where(inside, 0.0, -1e30)
    first = lane_index(1, LANES) < HEAD

    for pair in range(HEADS // 2):
        lanes = slice(pair * LANES, (pair + 1) * LANES)
        for tile in range(ROWS // TILE):
            rows = slice(tile * TILE, (tile + 1) * TILE)
            window = slice(tile * TILE, tile * TILE + WINDOW)
            queries = q_ref[ROWS + tile * TILE : ROWS + (tile + 1) * TILE, lanes]
            keys = k_ref[window, lanes]
            values = v_ref[window, lanes]
            bias = bias_ref[tile]
            grads = []
            for mine, g_ref in ((first, g0_ref), (~first, g1_ref)):
                score = mm_t(jnp.where(mine, queries, jnp.zeros_like(queries)), keys)
                weight = jnp.exp2(score * exponent_scale + bias)
                pull = mm_t(g_ref[rows, lanes], jnp.where(mine, values, jnp.ones_like(values)))
                grads.append(mm((weight * pull).astype(bf16), keys))
            qgrad_ref[rows, lanes] = jnp.where(first, grads[0], grads[1]) * 0.125


def backward_kernel(
    place_ref, low_ref, high_ref, decoder_ref, wa_ref, wb_ref, q_ref, k_ref, v_ref,
    scaled_ref, g0_ref, g1_ref, reach_ref, qgrad_ref, unit_ref, factor_ref,
    qkv_grad_ref,
    all_scaled, all_g0, all_g1, all_reach, bias_ref, grad_ref, kv_ref,
):
    row, lane = pick(LANES, INNER)
    spread = lambda start: row == start + lane // HEAD
    expand_total = jnp.where(spread(VARS) | spread(VARS + 8), 1.0, 0.0).astype(bf16)
    expand_dot = jnp.where(spread(VARS + 16), 1.0, 0.0).astype(bf16)
    middle = slice(ROWS, 2 * ROWS)
    all_scaled[middle, :] = scaled_ref[...]
    all_g0[middle, :] = g0_ref[...]
    all_g1[middle, :] = g1_ref[...]
    all_reach[:, middle] = jnp.broadcast_to(reach_ref[...], (8, ROWS))
    for block, message_ref in ((0, low_ref), (2, high_ref)):
        rows = slice(block * ROWS, (block + 1) * ROWS)
        message = message_ref[...]
        turned = message.astype(f32).T
        all_reach[:, rows] = jnp.broadcast_to(turned[REACH_LANE : REACH_LANE + 1, :], (8, ROWS)).astype(jnp.int32)
        grad = mixed_gradient(
            mm(message, decoder_ref[...]).astype(bf16), place_ref, wa_ref, wb_ref, grad_ref
        )
        total = mm(message, expand_total)
        scaled = (grad / jnp.where(total > 0.0, total, 1.0)).astype(bf16)
        all_scaled[rows, :] = scaled
        gradient_operands(scaled, mm(message, expand_dot), all_g0, all_g1, rows)

    for tile in range(ROWS // TILE):
        offset = (
            HALF
            + lax.broadcasted_iota(jnp.int32, (TILE, WINDOW), 0)
            - lane_index(TILE, WINDOW)
        )
        reach = all_reach[0:1, tile * TILE : tile * TILE + WINDOW]
        bias_ref[tile] = jnp.where((offset >= -reach) & (offset < reach), 0.0, -1e30)
    first = lane_index(1, LANES) < HEAD

    for pair in range(HEADS // 2):
        lanes = slice(pair * LANES, (pair + 1) * LANES)
        value_lanes = slice(INNER + pair * LANES, INNER + (pair + 1) * LANES)
        for tile in range(ROWS // TILE):
            rows = slice(tile * TILE, (tile + 1) * TILE)
            window = slice(tile * TILE, tile * TILE + WINDOW)
            keys = k_ref[ROWS + tile * TILE : ROWS + (tile + 1) * TILE, lanes]
            values = v_ref[ROWS + tile * TILE : ROWS + (tile + 1) * TILE, lanes]
            queries = q_ref[window, lanes]
            scaled = all_scaled[window, lanes]
            bias = bias_ref[tile]
            key_grads = []
            value_grads = []
            for mine, g_ref in ((first, all_g0), (~first, all_g1)):
                score = mm_t(jnp.where(mine, keys, jnp.zeros_like(keys)), queries)
                weight = jnp.exp2(score * exponent_scale + bias)
                pull = mm_t(jnp.where(mine, values, jnp.ones_like(values)), g_ref[window, lanes])
                value_grads.append(mm(weight.astype(bf16), scaled))
                key_grads.append(mm((weight * pull).astype(bf16), queries))
            kv_ref[rows, lanes] = jnp.where(first, key_grads[0], key_grads[1]) * 0.125
            kv_ref[rows, value_lanes] = jnp.where(first, value_grads[0], value_grads[1])

    segments = segment_matrix(1.0 / HEAD)
    for part, grad in ((0, qgrad_ref[...]), (1, kv_ref[:, :INNER])):
        columns = slice(part * INNER, (part + 1) * INNER)
        unit = unit_ref[:, columns]
        along = head_means(grad * unit, segments)
        qkv_grad_ref[:, columns] = (factor_ref[:, columns] * (grad - unit * along)).astype(bf16)
    qkv_grad_ref[:, 2 * INNER :] = kv_ref[:, INNER:].astype(bf16)


def hidden_kernel(
    place_ref, qkv_grad_ref, wa_ref, wb_ref, latent_ref, pert_ref, gain_ref, upd_ref, loss_ref,
    noise_ref, send_ref, normed_grad_ref,
):
    parts = [qkv_grad_ref[:, part * INNER : (part + 1) * INNER] for part in range(3)]
    for w_ref, lanes in zip((wa_ref, wb_ref), core_halves(place_ref, INNER)):
        normed_grad_ref[:, lanes] = (
            mm_t(parts[0], qkv_weights(w_ref, 0))
            + mm_t(parts[1], qkv_weights(w_ref, 1))
            + mm_t(parts[2], qkv_weights(w_ref, 2))
        )
    gain = gain_ref[...].astype(f32)
    for part in range(ROWS // TILE):
        rows = slice(part * TILE, (part + 1) * TILE)
        hidden = latent_ref[rows, :].astype(f32) + pert_ref[rows, :].astype(f32)
        centred = hidden - jnp.mean(hidden, axis=1, keepdims=True)
        inverse = lax.rsqrt(jnp.mean(centred * centred, axis=1, keepdims=True) + norm_epsilon)
        standard = centred * inverse
        grad = normed_grad_ref[rows, :] * gain
        first_term = jnp.mean(grad, axis=1, keepdims=True)
        second_term = standard * jnp.mean(grad * standard, axis=1, keepdims=True)
        result = upd_ref[rows, :] + inverse * (grad - first_term - second_term)
        noise_ref[rows, :] = result
        turned = result.T.astype(bf16)
        for member in range(MEMBERS):
            send_ref[member, :HEAD, rows] = turned[member * HEAD : (member + 1) * HEAD, :]
    loss = jnp.broadcast_to(loss_ref[0:1, 0:1], (16, ROWS))
    high, middle = split(loss)
    low = (loss - high.astype(f32) - middle.astype(f32)).astype(bf16)
    lanes = lane_index(16, ROWS)
    tail = jnp.zeros((16, ROWS), f32)
    for lane, part in enumerate((high, middle, low)):
        tail = jnp.where(lanes == lane, part.astype(f32), tail)
    for member in range(MEMBERS):
        send_ref[member, HEAD:, :] = tail.astype(bf16)


def finish_kernel(received_ref, latent_grad_ref, loss_ref):
    total = received_ref[0].astype(f32)
    for member in range(1, MEMBERS):
        total = total + received_ref[member].astype(f32)
    latent_grad_ref[...] = total[:HEAD]
    loss_ref[...] = jnp.broadcast_to(jnp.sum(total[HEAD : HEAD + 1, :], axis=1, keepdims=True), (8, LANES))


def call(body, outs, scratch, megabytes, cost, *operands, far=()):
    spaces = [
        pltpu.SMEM if o.dtype == jnp.int32 and o.ndim == 1 else pltpu.HBM if i in far else pltpu.VMEM
        for i, o in enumerate(operands)
    ]
    specs = [pl.BlockSpec(memory_space=space) for space in spaces]
    semaphores = [pltpu.SemaphoreType.DMA((len(far),))] if far else []
    result = pl.pallas_call(
        body,
        out_shape=tuple(jax.ShapeDtypeStruct(shape, kind) for shape, kind in outs),
        in_specs=specs,
        out_specs=tuple(pl.BlockSpec(memory_space=pltpu.VMEM) for _ in outs),
        scratch_shapes=[pltpu.VMEM(shape, kind) for shape, kind in scratch] + semaphores,
        compiler_params=pltpu.CompilerParams(vmem_limit_bytes=megabytes * 1024 * 1024),
        cost_estimate=pl.CostEstimate(flops=cost, bytes_accessed=4_000_000, transcendentals=0),
    )(*operands)
    return result


def both_ways(block):
    count = lax.axis_size(NODE)
    low = lax.ppermute(block, NODE, [(i, i + 1) for i in range(count - 1)])
    high = lax.ppermute(block, NODE, [(i + 1, i) for i in range(count - 1)])
    return low, high


def flat(y, xl, c, z, xh):
    return (((y * 2 + xl) * 2 + c) * 16 + z) * 2 + xh


def rank(y, xl, c):
    return c * 8 + y * 2 + xl


def members():
    return [(y, xl, c) for y in range(4) for xl in range(2) for c in range(2)]


def weight_route():
    by_rank = {rank(*member): member for member in members()}
    pairs = []
    for member in members():
        for z in range(16):
            for xh in range(2):
                source = flat(*by_rank[z], rank(*member), xh)
                pairs.append((source, flat(*member, z, xh)))
    return pairs


def loss_route():
    pairs = []
    for shift, member in enumerate(members()):
        for z in range(16):
            for xh in range(2):
                pairs.append((flat(*member, z, xh), flat(*member, (z + shift) % 16, xh)))
    return pairs


def shards(
    latent,
    member_perturbations,
    layer_norm_gain,
    query_key_value_weight,
    output_weight_matrix,
    decoder_weight_matrix,
    observed_truth,
    region_mask,
    node_window_halfspan,
):
    pert = member_perturbations[0]
    node_total = ROWS * lax.axis_size(NODE)
    member = lax.axis_index(MEMBER)
    place = jnp.stack([lax.axis_index(NODE) * ROWS, jnp.int32(node_total), lax.axis_index("c"), lax.axis_index("xh")]).astype(jnp.int32)

    packed = jnp.concatenate(
        [
            query_key_value_weight,
            jnp.concatenate([output_weight_matrix[:, :INNER], output_weight_matrix[:, INNER:]], axis=0),
        ],
        axis=1,
    )
    with jax.named_scope("weights_over_node"):
        mine = lax.ppermute(packed, EVERY, weight_route())
    decoder = jnp.pad(decoder_weight_matrix, ((0, LANES - VARS), (0, 0)))
    truth = lax.dynamic_slice_in_dim(observed_truth, member * SLOT, SLOT, 1)
    truth = jnp.pad(truth.T, ((0, 0), (0, LANES - VARS)))
    mask = lax.dynamic_slice_in_dim(region_mask, member * SLOT, SLOT, 0)
    area = (1.0 - (1.0 - region_share) * mask.astype(f32))[:, None]
    area = jnp.broadcast_to(area, (SLOT, LANES))
    latent_copies = jnp.broadcast_to(latent.T[None], (MEMBERS, HEAD, ROWS))
    place, reach_row, decoder, truth, area, gain, latent_copies = lax.optimization_barrier(
        (place, node_window_halfspan[None], decoder, truth, area,
         layer_norm_gain[None], latent_copies)
    )
    with jax.named_scope("latent_over_member"):
        latent_turned = lax.all_to_all(latent_copies, MEMBER, 0, 0, tiled=True).reshape(WIDTH, ROWS)
    with jax.named_scope("layer_norm"):
        normed, latent_own = call(
            norm_kernel,
            [((ROWS, WIDTH), bf16), ((ROWS, WIDTH), bf16)],
            [],
            8,
            1_000_000_000,
            latent_turned, pert, gain,
        )
    mine, normed = lax.optimization_barrier((mine, normed))
    with jax.named_scope("normed_halo"):
        normed_low, normed_high = both_ways(normed)
    with jax.named_scope("weights_over_x"):
        row = lax.all_to_all(jnp.broadcast_to(mine[None], (4,) + mine.shape), ("xl", "xh"), 0, 0, tiled=True)
        row = row.reshape(128, PACKED)
    with jax.named_scope("weights_over_y"):
        wa = lax.all_to_all(jnp.broadcast_to(row[None], (4,) + row.shape), "y", 0, 0, tiled=True)
        wa = wa.reshape(16, 32, PACKED)
    wa, normed_low, normed_high = lax.optimization_barrier((wa, normed_low, normed_high))
    with jax.named_scope("normed_rows"):
        normed_all = jnp.concatenate([normed_low, normed, normed_high], axis=0)
    with jax.named_scope("weights_over_core"):
        wb = lax.ppermute(wa, "c", [(0, 1), (1, 0)])
    with jax.named_scope("forward"):
        q, k, v, unit, factor, mixed, total, forecast = call(
            forward_kernel,
            [((EXT, INNER), bf16)] * 3
            + [((ROWS, WIDTH), f32)] * 2
            + [((ROWS, INNER), f32)] * 2
            + [((ROWS, LANES), f32)],
            [((2, TILE, WINDOW), f32), ((ROWS, INNER), bf16)],
            40,
            4_000_000_000,
            place, normed_all, wa, wb, latent_own, pert, reach_row, decoder,
        )
    with jax.named_scope("forecasts_over_member"):
        forecasts = lax.all_to_all(
            forecast.reshape(MEMBERS, SLOT, LANES), MEMBER, 0, 0, tiled=True
        )
    with jax.named_scope("score"):
        (pred_grads,) = call(
            score_kernel, [((MEMBERS, SLOT, LANES), bf16)], [], 8, 10_000_000, forecasts, truth, area
        )
    with jax.named_scope("gradients_over_member"):
        pred_grad = lax.all_to_all(pred_grads, MEMBER, 0, 0, tiled=True).reshape(ROWS, LANES)
    with jax.named_scope("upstream"):
        upd, scaled, g0, g1, message, loss_part = call(
            upstream_kernel,
            [((ROWS, WIDTH), f32)] + [((ROWS, INNER), bf16)] * 3 + [((ROWS, LANES), bf16), ((8, LANES), f32)],
            [((ROWS, INNER), f32)],
            16,
            500_000_000,
            place, pred_grad, decoder, wa, wb, mixed, total, reach_row,
        )
    with jax.named_scope("gradient_halo"):
        message_low, message_high = both_ways(message)
    with jax.named_scope("query_gradients"):
        (qgrad,) = call(
            query_kernel,
            [((ROWS, INNER), f32)],
            [((2, TILE, WINDOW), f32)],
            12,
            4_000_000_000,
            place, q, k, v, g0, g1, reach_row,
        )
    with jax.named_scope("loss_over_node"):
        (loss_part,) = call(
            pair_kernel, [((8, LANES), f32)], [], 4, 10_000, place, loss_part, message_low, message_high
        )
        loss_part = lax.ppermute(loss_part, EVERY, loss_route())
    with jax.named_scope("backward"):
        (qkv_grad,) = call(
            backward_kernel,
            [((ROWS, 3 * INNER), bf16)],
            [((EXT, INNER), bf16)] * 3
            + [((8, EXT), jnp.int32)]
            + [((2, TILE, WINDOW), f32), ((ROWS, INNER), f32), ((ROWS, WIDTH), f32)],
            24,
            4_000_000_000,
            place, message_low, message_high, decoder, wa, wb, q, k, v, scaled, g0, g1, reach_row,
            qgrad, unit, factor,
        )
    with jax.named_scope("hidden_gradient"):
        noise, send = call(
            hidden_kernel,
            [((ROWS, WIDTH), f32), ((MEMBERS, HEAD + 16, ROWS), bf16)],
            [((ROWS, WIDTH), f32)],
            16,
            1_000_000_000,
            place, qkv_grad, wa, wb, latent_own, pert, gain, upd, loss_part,
        )
    with jax.named_scope("latent_gradient_over_member"):
        received = lax.all_to_all(send, MEMBER, 0, 0, tiled=True)
    with jax.named_scope("finish"):
        latent_grad, loss = call(
            finish_kernel, [((HEAD, ROWS), f32), ((8, LANES), f32)], [], 8, 10_000_000, received
        )
    loss = loss[0, 0] / (MEMBERS * node_total * VARS)
    return (loss, latent_grad.T, noise[None])


def solution(mesh):
    fine = Mesh(mesh.devices.reshape(4, 2, 2, 16, 2), EVERY)
    placed = (
        P(NODE, MEMBER),
        P(MEMBER, NODE, None),
        P(),
        P(NODE, None),
        P(NODE, None),
        P(),
        P(None, NODE),
        P(NODE),
        P(NODE),
    )
    return jax.shard_map(
        shards,
        mesh=fine,
        in_specs=placed,
        out_specs=(P(), P(NODE, MEMBER), P(MEMBER, NODE, None)),
        check_vma=False,
    )
```

```python
import functools
import math

import jax
import jax.numpy as jnp
from jax import lax
from jax.experimental import pallas as pl
from jax.experimental.pallas import tpu as pltpu
from jax.sharding import Mesh, PartitionSpec as P

HEADS = 8
HEAD = 64
INNER = 512
ROWS = 256
HALF = 256
EXT = ROWS + 2 * HALF
WIDTH = 1024
VARS = 98
LANES = 128
MEMBERS = 16
SLOT = ROWS // MEMBERS
TILE = 256
WINDOW = TILE + 2 * HALF
LOSS_LANE = 122
REACH_LANE = 125
BLOCK = 256
PACKED = 2048

norm_epsilon = 1e-05
head_epsilon = 1e-06
smooth_width = 0.1
region_share = 0.25
exponent_scale = math.log2(math.e) / 8.0

MEMBER = ("y", "xl", "c")
NODE = ("z", "xh")
EVERY = MEMBER + NODE

bf16 = jnp.bfloat16
f32 = jnp.float32


def mm(left, right):
    return lax.dot_general(left, right, (((1,), (0,)), ((), ())), preferred_element_type=f32)


def mm_t(left, right):
    return lax.dot_general(left, right, (((1,), (1,)), ((), ())), preferred_element_type=f32)


def split(value):
    high = value.astype(bf16)
    return high, (value - high.astype(f32)).astype(bf16)


def segment_matrix(scale):
    rows = lax.broadcasted_iota(jnp.int32, (BLOCK, BLOCK), 0) // HEAD
    columns = lax.broadcasted_iota(jnp.int32, (BLOCK, BLOCK), 1) // HEAD
    return jnp.where(rows == columns, scale, 0.0).astype(bf16)


def head_sums(value, segments):
    high, low = split(value)
    parts = []
    for start in range(0, INNER, BLOCK):
        lanes = slice(start, start + BLOCK)
        parts.append(mm(high[:, lanes], segments) + mm(low[:, lanes], segments))
    return jnp.concatenate(parts, axis=1)


def head_means(value, segments):
    rounded = value.astype(bf16)
    return jnp.concatenate(
        [mm(rounded[:, start : start + BLOCK], segments) for start in range(0, INNER, BLOCK)], axis=1
    )


def lane_index(rows, lanes):
    return lax.broadcasted_iota(jnp.int32, (rows, lanes), 1)


def norm_kernel(lat_ref, pert_ref, gain_ref, normed_ref, latent_ref):
    gain = gain_ref[...].astype(f32)
    for part in range(ROWS // TILE):
        rows = slice(part * TILE, (part + 1) * TILE)
        lat = lat_ref[:, rows].astype(f32).T
        latent_ref[rows, :] = lat.astype(bf16)
        hidden = lat + pert_ref[rows, :].astype(f32)
        centred = hidden - jnp.mean(hidden, axis=1, keepdims=True)
        inverse = lax.rsqrt(jnp.mean(centred * centred, axis=1, keepdims=True) + norm_epsilon)
        normed_ref[rows, :] = (centred * inverse * gain).astype(bf16)


def out_weights(w_ref, side):
    rows = slice(side * 16, side * 16 + 16)
    return w_ref[:, rows, 3 * INNER :].reshape(INNER // 2, INNER)


def qkv_weights(w_ref, part):
    return w_ref[:, :, part * INNER : (part + 1) * INNER].reshape(INNER, INNER)


def core_halves(place_ref, size):
    core = place_ref[2]
    return (
        pl.ds(pl.multiple_of(core * size, size), size),
        pl.ds(pl.multiple_of((1 - core) * size, size), size),
    )


def column_of(row_ref):
    row = jnp.broadcast_to(row_ref[...].astype(f32), (LANES, ROWS))
    return row.T.astype(jnp.int32)


def forward_kernel(
    place_ref, normed_ref, wa_ref, wb_ref, latent_ref, pert_ref, reach_ref, decoder_ref,
    q_ref, k_ref, v_ref, unit_ref, factor_ref, mixed_ref, total_ref, forecast_ref,
    bias_ref, mixed_low_ref,
):
    row_start = place_ref[0]
    segments = segment_matrix(1.0 / HEAD)
    near, far = core_halves(place_ref, INNER)
    for block in range(3):
        rows = slice(block * ROWS, (block + 1) * ROWS)
        left, right = normed_ref[rows, near], normed_ref[rows, far]
        together = mm(left, wa_ref[:, :, : 3 * INNER].reshape(INNER, 3 * INNER)) + mm(
            right, wb_ref[:, :, : 3 * INNER].reshape(INNER, 3 * INNER)
        )
        for part, out_ref in enumerate((q_ref, k_ref, v_ref)):
            projected = together[:, part * INNER : (part + 1) * INNER]
            if part < 2:
                factor = lax.rsqrt(head_means(projected * projected, segments) + head_epsilon)
                unit = projected * factor
                if block == 1:
                    unit_ref[:, part * INNER : (part + 1) * INNER] = unit
                    factor_ref[:, part * INNER : (part + 1) * INNER] = factor
                projected = unit
            out_ref[rows, :] = projected.astype(bf16)

    column = column_of(reach_ref)
    for tile in range(ROWS // TILE):
        offset = (
            lane_index(TILE, WINDOW)
            - HALF
            - lax.broadcasted_iota(jnp.int32, (TILE, WINDOW), 0)
        )
        position = row_start - HALF + tile * TILE + lane_index(TILE, WINDOW)
        reach = column[tile * TILE : (tile + 1) * TILE, 0:1]
        inside = (offset >= -reach) & (offset < reach) & (position >= 0) & (position < place_ref[1])
        bias_ref[tile] = jnp.where(inside, 0.0, -1e30)

    first = lane_index(1, LANES) < HEAD

    for pair in range(HEADS // 2):
        lanes = slice(pair * LANES, (pair + 1) * LANES)
        for tile in range(ROWS // TILE):
            rows = slice(tile * TILE, (tile + 1) * TILE)
            window = slice(tile * TILE, tile * TILE + WINDOW)
            queries = q_ref[ROWS + tile * TILE : ROWS + (tile + 1) * TILE, lanes]
            keys = k_ref[window, lanes]
            values = v_ref[window, lanes]
            bias = bias_ref[tile]
            outs = []
            for mine in (first, ~first):
                score = mm_t(jnp.where(mine, queries, jnp.zeros_like(queries)), keys)
                weight = jnp.exp2(score * exponent_scale + bias).astype(bf16)
                outs.append(mm(weight, jnp.where(mine, values, jnp.ones_like(values))))
            total = pltpu.roll(jnp.where(first, outs[1], outs[0]), HEAD, 1)
            mixed = jnp.where(first, outs[0], outs[1]) / total
            mixed_ref[rows, lanes] = mixed
            mixed_low_ref[rows, lanes] = mixed.astype(bf16)
            total_ref[rows, lanes] = total

    near, far = core_halves(place_ref, INNER // 2)
    left, right = mixed_low_ref[:, near], mixed_low_ref[:, far]
    forecast = jnp.zeros((ROWS, LANES), f32)
    for side in range(2):
        columns = slice(side * INNER, (side + 1) * INNER)
        branch = mm(left, out_weights(wa_ref, side)) + mm(right, out_weights(wb_ref, side))
        hidden = latent_ref[:, columns].astype(f32) + pert_ref[:, columns].astype(f32)
        updated = (hidden + branch).astype(bf16)
        forecast = forecast + mm_t(updated, decoder_ref[:, columns])
    forecast_ref[...] = forecast


def score_kernel(forecast_ref, truth_ref, area_ref, out_ref):
    lanes = lane_index(SLOT, LANES)
    area = jnp.where(lanes < VARS, area_ref[...], 0.0)
    truth = truth_ref[...]
    square = smooth_width * smooth_width
    loss = jnp.zeros((SLOT, LANES), f32)
    for member in range(MEMBERS):
        own = forecast_ref[member]
        pull = jnp.zeros((SLOT, LANES), f32)
        spread = jnp.zeros((SLOT, LANES), f32)
        for other in range(MEMBERS):
            if other == member:
                continue
            gap = own - forecast_ref[other]
            power = gap * gap + square
            inverse = lax.rsqrt(power)
            pull = pull + gap * inverse
            spread = spread + power * inverse
        gap = own - truth
        power = gap * gap + square
        inverse = lax.rsqrt(power)
        loss = loss + area * (power * inverse - spread * (0.5 / (MEMBERS - 1)))
        out_ref[member] = (area * (gap * inverse - pull * (1.0 / (MEMBERS - 1)))).astype(bf16)
    total = jnp.sum(jnp.sum(loss, axis=1, keepdims=True), axis=0, keepdims=True)
    total = jnp.broadcast_to(total, (SLOT, LANES))
    high, rest = split(total)
    middle = rest
    low = (total - high.astype(f32) - middle.astype(f32)).astype(bf16)
    for member in range(MEMBERS):
        kept = out_ref[member]
        kept = jnp.where(lanes == VARS, high, kept)
        kept = jnp.where(lanes == VARS + 1, middle, kept)
        out_ref[member] = jnp.where(lanes == VARS + 2, low, kept)


def mixed_gradient(upd_low, place_ref, wa_ref, wb_ref, target_ref):
    for w_ref, lanes in zip((wa_ref, wb_ref), core_halves(place_ref, INNER // 2)):
        target_ref[:, lanes] = mm_t(upd_low[:, :INNER], out_weights(w_ref, 0)) + mm_t(
            upd_low[:, INNER:], out_weights(w_ref, 1)
        )
    return target_ref[...].astype(bf16).astype(f32)


def gradient_operands(scaled, row_dot, g0_ref, g1_ref, rows):
    first = lane_index(1, LANES) < HEAD
    spot = lane_index(ROWS, LANES) % HEAD
    for pair in range(HEADS // 2):
        lanes = slice(pair * LANES, (pair + 1) * LANES)
        high, low = split(-pltpu.roll(row_dot[:, lanes], HEAD, 1))
        zero = jnp.zeros_like(high)
        extra = jnp.where(spot == 0, high, jnp.where(spot == 1, low, zero))
        own = scaled[:, lanes]
        g0_ref[rows, lanes] = jnp.where(first, own, extra)
        g1_ref[rows, lanes] = jnp.where(first, extra, own)


def pick(rows, lanes):
    row = lax.broadcasted_iota(jnp.int32, (rows, lanes), 0)
    lane = lane_index(rows, lanes)
    return row, lane


def upstream_kernel(
    place_ref, pg_ref, decoder_ref, wa_ref, wb_ref, mixed_ref, total_ref, reach_ref,
    upd_ref, scaled_ref, g0_ref, g1_ref, message_ref, loss_ref, grad_ref,
):
    pg = pg_ref[...]
    upd = mm(pg, decoder_ref[...])
    upd_ref[...] = upd
    everything = slice(0, ROWS)
    grad = mixed_gradient(upd.astype(bf16), place_ref, wa_ref, wb_ref, grad_ref)
    total = total_ref[...]
    inverse = 1.0 / total
    row_dot = head_sums(grad * mixed_ref[...], segment_matrix(1.0)) * inverse
    scaled = (grad * inverse).astype(bf16)
    scaled_ref[...] = scaled
    gradient_operands(scaled, row_dot, g0_ref, g1_ref, everything)

    row, lane = pick(INNER, LANES)
    head_row = (row % HEAD == 0)
    chosen = lambda start: jnp.where(head_row & (lane == start + row // HEAD), 1.0, 0.0).astype(bf16)
    high, low = split(total)
    stats = mm(high, chosen(VARS)) + mm(low, chosen(VARS + 8)) + mm(row_dot.astype(bf16), chosen(VARS + 16))
    lanes = lane_index(ROWS, LANES)
    message = jnp.where(lanes < VARS, pg.astype(f32), stats)
    message = jnp.where(lanes == REACH_LANE, column_of(reach_ref).astype(f32), message)
    kept = jnp.where((lanes >= VARS) & (lanes < VARS + 3), pg.astype(f32), 0.0)
    loss = jnp.sum(jnp.sum(kept, axis=1, keepdims=True), axis=0, keepdims=True) * (1.0 / SLOT)
    loss_ref[...] = jnp.broadcast_to(loss, (8, LANES))
    high, middle = split(loss)
    low = (loss - high.astype(f32) - middle.astype(f32)).astype(bf16)
    for lane, part in enumerate((high, middle, low)):
        message = jnp.where(lanes == LOSS_LANE + lane, part.astype(f32), message)
    message_ref[...] = message.astype(bf16)


def pair_kernel(place_ref, own_ref, low_ref, high_ref, out_ref):
    lanes = lane_index(1, LANES)
    even = place_ref[3] == 0
    nearby = jnp.where(even, high_ref[0:16, :].astype(f32), low_ref[0:16, :].astype(f32))[0:1, :]
    nearby = jnp.where((lanes >= LOSS_LANE) & (lanes < LOSS_LANE + 3), nearby, 0.0)
    out_ref[...] = own_ref[...] + jnp.sum(nearby, axis=1, keepdims=True)


def query_kernel(
    place_ref, q_ref, k_ref, v_ref, g0_ref, g1_ref, reach_ref, qgrad_ref, bias_ref,
):
    row_start = place_ref[0]
    column = column_of(reach_ref)
    for tile in range(ROWS // TILE):
        offset = (
            lane_index(TILE, WINDOW)
            - HALF
            - lax.broadcasted_iota(jnp.int32, (TILE, WINDOW), 0)
        )
        position = row_start - HALF + tile * TILE + lane_index(TILE, WINDOW)
        reach = column[tile * TILE : (tile + 1) * TILE, 0:1]
        inside = (offset >= -reach) & (offset < reach) & (position >= 0) & (position < place_ref[1])
        bias_ref[tile] = jnp.where(inside, 0.0, -1e30)
    first = lane_index(1, LANES) < HEAD

    for pair in range(HEADS // 2):
        lanes = slice(pair * LANES, (pair + 1) * LANES)
        for tile in range(ROWS // TILE):
            rows = slice(tile * TILE, (tile + 1) * TILE)
            window = slice(tile * TILE, tile * TILE + WINDOW)
            queries = q_ref[ROWS + tile * TILE : ROWS + (tile + 1) * TILE, lanes]
            keys = k_ref[window, lanes]
            values = v_ref[window, lanes]
            bias = bias_ref[tile]
            grads = []
            for mine, g_ref in ((first, g0_ref), (~first, g1_ref)):
                score = mm_t(jnp.where(mine, queries, jnp.zeros_like(queries)), keys)
                weight = jnp.exp2(score * exponent_scale + bias)
                pull = mm_t(g_ref[rows, lanes], jnp.where(mine, values, jnp.ones_like(values)))
                grads.append(mm((weight * pull).astype(bf16), keys))
            qgrad_ref[rows, lanes] = jnp.where(first, grads[0], grads[1]) * 0.125


def backward_kernel(
    place_ref, low_ref, high_ref, decoder_ref, wa_ref, wb_ref, q_ref, k_ref, v_ref,
    scaled_ref, g0_ref, g1_ref, reach_ref, qgrad_ref, unit_ref, factor_ref,
    qkv_grad_ref,
    all_scaled, all_g0, all_g1, all_reach, bias_ref, grad_ref, kv_ref,
):
    row, lane = pick(LANES, INNER)
    spread = lambda start: row == start + lane // HEAD
    expand_total = jnp.where(spread(VARS) | spread(VARS + 8), 1.0, 0.0).astype(bf16)
    expand_dot = jnp.where(spread(VARS + 16), 1.0, 0.0).astype(bf16)
    middle = slice(ROWS, 2 * ROWS)
    all_scaled[middle, :] = scaled_ref[...]
    all_g0[middle, :] = g0_ref[...]
    all_g1[middle, :] = g1_ref[...]
    all_reach[:, middle] = jnp.broadcast_to(reach_ref[...], (8, ROWS))
    for block, message_ref in ((0, low_ref), (2, high_ref)):
        rows = slice(block * ROWS, (block + 1) * ROWS)
        message = message_ref[...]
        turned = message.astype(f32).T
        all_reach[:, rows] = jnp.broadcast_to(turned[REACH_LANE : REACH_LANE + 1, :], (8, ROWS)).astype(jnp.int32)
        grad = mixed_gradient(
            mm(message, decoder_ref[...]).astype(bf16), place_ref, wa_ref, wb_ref, grad_ref
        )
        total = mm(message, expand_total)
        scaled = (grad / jnp.where(total > 0.0, total, 1.0)).astype(bf16)
        all_scaled[rows, :] = scaled
        gradient_operands(scaled, mm(message, expand_dot), all_g0, all_g1, rows)

    for tile in range(ROWS // TILE):
        offset = (
            HALF
            + lax.broadcasted_iota(jnp.int32, (TILE, WINDOW), 0)
            - lane_index(TILE, WINDOW)
        )
        reach = all_reach[0:1, tile * TILE : tile * TILE + WINDOW]
        bias_ref[tile] = jnp.where((offset >= -reach) & (offset < reach), 0.0, -1e30)
    first = lane_index(1, LANES) < HEAD

    for pair in range(HEADS // 2):
        lanes = slice(pair * LANES, (pair + 1) * LANES)
        value_lanes = slice(INNER + pair * LANES, INNER + (pair + 1) * LANES)
        for tile in range(ROWS // TILE):
            rows = slice(tile * TILE, (tile + 1) * TILE)
            window = slice(tile * TILE, tile * TILE + WINDOW)
            keys = k_ref[ROWS + tile * TILE : ROWS + (tile + 1) * TILE, lanes]
            values = v_ref[ROWS + tile * TILE : ROWS + (tile + 1) * TILE, lanes]
            queries = q_ref[window, lanes]
            scaled = all_scaled[window, lanes]
            bias = bias_ref[tile]
            key_grads = []
            value_grads = []
            for mine, g_ref in ((first, all_g0), (~first, all_g1)):
                score = mm_t(jnp.where(mine, keys, jnp.zeros_like(keys)), queries)
                weight = jnp.exp2(score * exponent_scale + bias)
                pull = mm_t(jnp.where(mine, values, jnp.ones_like(values)), g_ref[window, lanes])
                value_grads.append(mm(weight.astype(bf16), scaled))
                key_grads.append(mm((weight * pull).astype(bf16), queries))
            kv_ref[rows, lanes] = jnp.where(first, key_grads[0], key_grads[1]) * 0.125
            kv_ref[rows, value_lanes] = jnp.where(first, value_grads[0], value_grads[1])

    segments = segment_matrix(1.0 / HEAD)
    for part, grad in ((0, qgrad_ref[...]), (1, kv_ref[:, :INNER])):
        columns = slice(part * INNER, (part + 1) * INNER)
        unit = unit_ref[:, columns]
        along = head_means(grad * unit, segments)
        qkv_grad_ref[:, columns] = (factor_ref[:, columns] * (grad - unit * along)).astype(bf16)
    qkv_grad_ref[:, 2 * INNER :] = kv_ref[:, INNER:].astype(bf16)


def hidden_kernel(
    place_ref, qkv_grad_ref, wa_ref, wb_ref, latent_ref, pert_ref, gain_ref, upd_ref, loss_ref,
    noise_ref, send_ref, normed_grad_ref,
):
    parts = [qkv_grad_ref[:, part * INNER : (part + 1) * INNER] for part in range(3)]
    for w_ref, lanes in zip((wa_ref, wb_ref), core_halves(place_ref, INNER)):
        normed_grad_ref[:, lanes] = (
            mm_t(parts[0], qkv_weights(w_ref, 0))
            + mm_t(parts[1], qkv_weights(w_ref, 1))
            + mm_t(parts[2], qkv_weights(w_ref, 2))
        )
    gain = gain_ref[...].astype(f32)
    for part in range(ROWS // TILE):
        rows = slice(part * TILE, (part + 1) * TILE)
        hidden = latent_ref[rows, :].astype(f32) + pert_ref[rows, :].astype(f32)
        centred = hidden - jnp.mean(hidden, axis=1, keepdims=True)
        inverse = lax.rsqrt(jnp.mean(centred * centred, axis=1, keepdims=True) + norm_epsilon)
        standard = centred * inverse
        grad = normed_grad_ref[rows, :] * gain
        first_term = jnp.mean(grad, axis=1, keepdims=True)
        second_term = standard * jnp.mean(grad * standard, axis=1, keepdims=True)
        result = upd_ref[rows, :] + inverse * (grad - first_term - second_term)
        noise_ref[rows, :] = result
        turned = result.T.astype(bf16)
        for member in range(MEMBERS):
            send_ref[member, :HEAD, rows] = turned[member * HEAD : (member + 1) * HEAD, :]
    loss = jnp.broadcast_to(loss_ref[0:1, 0:1], (16, ROWS))
    high, middle = split(loss)
    low = (loss - high.astype(f32) - middle.astype(f32)).astype(bf16)
    lanes = lane_index(16, ROWS)
    tail = jnp.zeros((16, ROWS), f32)
    for lane, part in enumerate((high, middle, low)):
        tail = jnp.where(lanes == lane, part.astype(f32), tail)
    for member in range(MEMBERS):
        send_ref[member, HEAD:, :] = tail.astype(bf16)


def finish_kernel(received_ref, latent_grad_ref, loss_ref):
    total = received_ref[0].astype(f32)
    for member in range(1, MEMBERS):
        total = total + received_ref[member].astype(f32)
    latent_grad_ref[...] = total[:HEAD]
    loss_ref[...] = jnp.broadcast_to(jnp.sum(total[HEAD : HEAD + 1, :], axis=1, keepdims=True), (8, LANES))


def call(body, outs, scratch, megabytes, cost, *operands, far=()):
    spaces = [
        pltpu.SMEM if o.dtype == jnp.int32 and o.ndim == 1 else pltpu.HBM if i in far else pltpu.VMEM
        for i, o in enumerate(operands)
    ]
    specs = [pl.BlockSpec(memory_space=space) for space in spaces]
    semaphores = [pltpu.SemaphoreType.DMA((len(far),))] if far else []
    result = pl.pallas_call(
        body,
        out_shape=tuple(jax.ShapeDtypeStruct(shape, kind) for shape, kind in outs),
        in_specs=specs,
        out_specs=tuple(pl.BlockSpec(memory_space=pltpu.VMEM) for _ in outs),
        scratch_shapes=[pltpu.VMEM(shape, kind) for shape, kind in scratch] + semaphores,
        compiler_params=pltpu.CompilerParams(vmem_limit_bytes=megabytes * 1024 * 1024),
        cost_estimate=pl.CostEstimate(flops=cost, bytes_accessed=4_000_000, transcendentals=0),
    )(*operands)
    return result


def both_ways(block):
    count = lax.axis_size(NODE)
    low = lax.ppermute(block, NODE, [(i, i + 1) for i in range(count - 1)])
    high = lax.ppermute(block, NODE, [(i + 1, i) for i in range(count - 1)])
    return low, high


def flat(y, xl, c, z, xh):
    return (((y * 2 + xl) * 2 + c) * 16 + z) * 2 + xh


def rank(y, xl, c):
    return c * 8 + y * 2 + xl


def members():
    return [(y, xl, c) for y in range(4) for xl in range(2) for c in range(2)]


def weight_route():
    by_rank = {rank(*member): member for member in members()}
    pairs = []
    for member in members():
        for z in range(16):
            for xh in range(2):
                source = flat(*by_rank[z], rank(*member), xh)
                pairs.append((source, flat(*member, z, xh)))
    return pairs


def loss_route():
    pairs = []
    for shift, member in enumerate(members()):
        for z in range(16):
            for xh in range(2):
                pairs.append((flat(*member, z, xh), flat(*member, (z + shift) % 16, xh)))
    return pairs


def shards(
    latent,
    member_perturbations,
    layer_norm_gain,
    query_key_value_weight,
    output_weight_matrix,
    decoder_weight_matrix,
    observed_truth,
    region_mask,
    node_window_halfspan,
):
    pert = member_perturbations[0]
    node_total = ROWS * lax.axis_size(NODE)
    member = lax.axis_index(MEMBER)
    place = jnp.stack([lax.axis_index(NODE) * ROWS, jnp.int32(node_total), lax.axis_index("c"), lax.axis_index("xh")]).astype(jnp.int32)

    packed = jnp.concatenate(
        [
            query_key_value_weight,
            jnp.concatenate([output_weight_matrix[:, :INNER], output_weight_matrix[:, INNER:]], axis=0),
        ],
        axis=1,
    )
    with jax.named_scope("weights_over_node"):
        mine = lax.ppermute(packed, EVERY, weight_route())
    latent_copies = jnp.broadcast_to(latent.T[None], (MEMBERS, HEAD, ROWS))
    with jax.named_scope("latent_over_member"):
        latent_turned = lax.all_to_all(latent_copies, MEMBER, 0, 0, tiled=True).reshape(WIDTH, ROWS)
    with jax.named_scope("layer_norm"):
        normed, latent_own = call(
            norm_kernel,
            [((ROWS, WIDTH), bf16), ((ROWS, WIDTH), bf16)],
            [],
            8,
            1_000_000_000,
            latent_turned, pert, layer_norm_gain[None],
        )
    (mine, normed, decoder_weight_matrix, observed_truth, region_mask, gain, reach_row, place) = (
        lax.optimization_barrier(
            (mine, normed, decoder_weight_matrix, observed_truth, region_mask, layer_norm_gain[None],
             node_window_halfspan[None], place)
        )
    )
    decoder = jnp.pad(decoder_weight_matrix, ((0, LANES - VARS), (0, 0)))
    truth = lax.dynamic_slice_in_dim(observed_truth, member * SLOT, SLOT, 1)
    truth = jnp.pad(truth.T, ((0, 0), (0, LANES - VARS)))
    mask = lax.dynamic_slice_in_dim(region_mask, member * SLOT, SLOT, 0)
    area = (1.0 - (1.0 - region_share) * mask.astype(f32))[:, None]
    area = jnp.broadcast_to(area, (SLOT, LANES))
    with jax.named_scope("normed_halo"):
        normed_low, normed_high = both_ways(normed)
    with jax.named_scope("weights_over_x"):
        row = lax.all_to_all(jnp.broadcast_to(mine[None], (4,) + mine.shape), ("xl", "xh"), 0, 0, tiled=True)
        row = row.reshape(128, PACKED)
    with jax.named_scope("weights_over_y"):
        wa = lax.all_to_all(jnp.broadcast_to(row[None], (4,) + row.shape), "y", 0, 0, tiled=True)
        wa = wa.reshape(16, 32, PACKED)
    wa, normed_low, normed_high, decoder, truth, area, gain, reach_row, place = lax.optimization_barrier(
        (wa, normed_low, normed_high, decoder, truth, area, gain, reach_row, place)
    )
    with jax.named_scope("normed_rows"):
        normed_all = jnp.concatenate([normed_low, normed, normed_high], axis=0)
    with jax.named_scope("weights_over_core"):
        wb = lax.ppermute(wa, "c", [(0, 1), (1, 0)])
    with jax.named_scope("forward"):
        q, k, v, unit, factor, mixed, total, forecast = call(
            forward_kernel,
            [((EXT, INNER), bf16)] * 3
            + [((ROWS, WIDTH), f32)] * 2
            + [((ROWS, INNER), f32)] * 2
            + [((ROWS, LANES), f32)],
            [((2, TILE, WINDOW), f32), ((ROWS, INNER), bf16)],
            40,
            4_000_000_000,
            place, normed_all, wa, wb, latent_own, pert, reach_row, decoder,
        )
    with jax.named_scope("forecasts_over_member"):
        forecasts = lax.all_to_all(
            forecast.reshape(MEMBERS, SLOT, LANES), MEMBER, 0, 0, tiled=True
        )
    with jax.named_scope("score"):
        (pred_grads,) = call(
            score_kernel, [((MEMBERS, SLOT, LANES), bf16)], [], 8, 10_000_000, forecasts, truth, area
        )
    with jax.named_scope("gradients_over_member"):
        pred_grad = lax.all_to_all(pred_grads, MEMBER, 0, 0, tiled=True).reshape(ROWS, LANES)
    with jax.named_scope("upstream"):
        upd, scaled, g0, g1, message, loss_part = call(
            upstream_kernel,
            [((ROWS, WIDTH), f32)] + [((ROWS, INNER), bf16)] * 3 + [((ROWS, LANES), bf16), ((8, LANES), f32)],
            [((ROWS, INNER), f32)],
            16,
            500_000_000,
            place, pred_grad, decoder, wa, wb, mixed, total, reach_row,
        )
    with jax.named_scope("gradient_halo"):
        message_low, message_high = both_ways(message)
    with jax.named_scope("query_gradients"):
        (qgrad,) = call(
            query_kernel,
            [((ROWS, INNER), f32)],
            [((2, TILE, WINDOW), f32)],
            12,
            4_000_000_000,
            place, q, k, v, g0, g1, reach_row,
        )
    with jax.named_scope("loss_over_node"):
        (loss_part,) = call(
            pair_kernel, [((8, LANES), f32)], [], 4, 10_000, place, loss_part, message_low, message_high
        )
        loss_part = lax.ppermute(loss_part, EVERY, loss_route())
    with jax.named_scope("backward"):
        (qkv_grad,) = call(
            backward_kernel,
            [((ROWS, 3 * INNER), bf16)],
            [((EXT, INNER), bf16)] * 3
            + [((8, EXT), jnp.int32)]
            + [((2, TILE, WINDOW), f32), ((ROWS, INNER), f32), ((ROWS, WIDTH), f32)],
            24,
            4_000_000_000,
            place, message_low, message_high, decoder, wa, wb, q, k, v, scaled, g0, g1, reach_row,
            qgrad, unit, factor,
        )
    with jax.named_scope("hidden_gradient"):
        noise, send = call(
            hidden_kernel,
            [((ROWS, WIDTH), f32), ((MEMBERS, HEAD + 16, ROWS), bf16)],
            [((ROWS, WIDTH), f32)],
            16,
            1_000_000_000,
            place, qkv_grad, wa, wb, latent_own, pert, gain, upd, loss_part,
        )
    with jax.named_scope("latent_gradient_over_member"):
        received = lax.all_to_all(send, MEMBER, 0, 0, tiled=True)
    with jax.named_scope("finish"):
        latent_grad, loss = call(
            finish_kernel, [((HEAD, ROWS), f32), ((8, LANES), f32)], [], 8, 10_000_000, received
        )
    loss = loss[0, 0] / (MEMBERS * node_total * VARS)
    return (loss, latent_grad.T, noise[None])


def solution(mesh):
    fine = Mesh(mesh.devices.reshape(4, 2, 2, 16, 2), EVERY)
    placed = (
        P(NODE, MEMBER),
        P(MEMBER, NODE, None),
        P(),
        P(NODE, None),
        P(NODE, None),
        P(),
        P(None, NODE),
        P(NODE),
        P(NODE),
    )
    return jax.shard_map(
        shards,
        mesh=fine,
        in_specs=placed,
        out_specs=(P(), P(NODE, MEMBER), P(MEMBER, NODE, None)),
        check_vma=False,
    )
```

```python
import functools
import math

import jax
import jax.numpy as jnp
from jax import lax
from jax.experimental import pallas as pl
from jax.experimental.pallas import tpu as pltpu
from jax.sharding import Mesh, PartitionSpec as P

HEADS = 8
HEAD = 64
INNER = 512
ROWS = 256
HALF = 256
EXT = ROWS + 2 * HALF
WIDTH = 1024
VARS = 98
LANES = 128
MEMBERS = 16
SLOT = ROWS // MEMBERS
TILE = 256
WINDOW = TILE + 2 * HALF
LOSS_LANE = 122
REACH_LANE = 125
BLOCK = 256
PACKED = 2048

norm_epsilon = 1e-05
head_epsilon = 1e-06
smooth_width = 0.1
region_share = 0.25
exponent_scale = math.log2(math.e) / 8.0

MEMBER = ("y", "xl", "c")
NODE = ("z", "xh")
EVERY = MEMBER + NODE

bf16 = jnp.bfloat16
f32 = jnp.float32


def mm(left, right):
    return lax.dot_general(left, right, (((1,), (0,)), ((), ())), preferred_element_type=f32)


def mm_t(left, right):
    return lax.dot_general(left, right, (((1,), (1,)), ((), ())), preferred_element_type=f32)


def split(value):
    high = value.astype(bf16)
    return high, (value - high.astype(f32)).astype(bf16)


def segment_matrix(scale):
    rows = lax.broadcasted_iota(jnp.int32, (BLOCK, BLOCK), 0) // HEAD
    columns = lax.broadcasted_iota(jnp.int32, (BLOCK, BLOCK), 1) // HEAD
    return jnp.where(rows == columns, scale, 0.0).astype(bf16)


def head_sums(value, segments):
    high, low = split(value)
    parts = []
    for start in range(0, INNER, BLOCK):
        lanes = slice(start, start + BLOCK)
        parts.append(mm(high[:, lanes], segments) + mm(low[:, lanes], segments))
    return jnp.concatenate(parts, axis=1)


def head_means(value, segments):
    rounded = value.astype(bf16)
    return jnp.concatenate(
        [mm(rounded[:, start : start + BLOCK], segments) for start in range(0, INNER, BLOCK)], axis=1
    )


def lane_index(rows, lanes):
    return lax.broadcasted_iota(jnp.int32, (rows, lanes), 1)


def norm_kernel(lat_ref, pert_ref, gain_ref, normed_ref, latent_ref):
    gain = gain_ref[...].astype(f32)
    for part in range(ROWS // TILE):
        rows = slice(part * TILE, (part + 1) * TILE)
        lat = lat_ref[:, rows].astype(f32).T
        latent_ref[rows, :] = lat.astype(bf16)
        hidden = lat + pert_ref[rows, :].astype(f32)
        centred = hidden - jnp.mean(hidden, axis=1, keepdims=True)
        inverse = lax.rsqrt(jnp.mean(centred * centred, axis=1, keepdims=True) + norm_epsilon)
        normed_ref[rows, :] = (centred * inverse * gain).astype(bf16)


def out_weights(w_ref, side):
    rows = slice(side * 16, side * 16 + 16)
    return w_ref[:, rows, 3 * INNER :].reshape(INNER // 2, INNER)


def qkv_weights(w_ref, part):
    return w_ref[:, :, part * INNER : (part + 1) * INNER].reshape(INNER, INNER)


def core_halves(place_ref, size):
    core = place_ref[2]
    return (
        pl.ds(pl.multiple_of(core * size, size), size),
        pl.ds(pl.multiple_of((1 - core) * size, size), size),
    )


def column_of(row_ref):
    row = jnp.broadcast_to(row_ref[...].astype(f32), (LANES, ROWS))
    return row.T.astype(jnp.int32)


def forward_kernel(
    place_ref, normed_ref, wa_ref, wb_ref, latent_ref, pert_ref, reach_ref, decoder_ref,
    q_ref, k_ref, v_ref, unit_ref, factor_ref, mixed_ref, total_ref, forecast_ref,
    bias_ref, mixed_low_ref,
):
    row_start = place_ref[0]
    segments = segment_matrix(1.0 / HEAD)
    near, far = core_halves(place_ref, INNER)
    for block in range(3):
        rows = slice(block * ROWS, (block + 1) * ROWS)
        left, right = normed_ref[rows, near], normed_ref[rows, far]
        together = mm(left, wa_ref[:, :, : 3 * INNER].reshape(INNER, 3 * INNER)) + mm(
            right, wb_ref[:, :, : 3 * INNER].reshape(INNER, 3 * INNER)
        )
        for part, out_ref in enumerate((q_ref, k_ref, v_ref)):
            projected = together[:, part * INNER : (part + 1) * INNER]
            if part < 2:
                factor = lax.rsqrt(head_means(projected * projected, segments) + head_epsilon)
                unit = projected * factor
                if block == 1:
                    unit_ref[:, part * INNER : (part + 1) * INNER] = unit
                    factor_ref[:, part * INNER : (part + 1) * INNER] = factor
                projected = unit
            out_ref[rows, :] = projected.astype(bf16)

    column = column_of(reach_ref)
    for tile in range(ROWS // TILE):
        offset = (
            lane_index(TILE, WINDOW)
            - HALF
            - lax.broadcasted_iota(jnp.int32, (TILE, WINDOW), 0)
        )
        position = row_start - HALF + tile * TILE + lane_index(TILE, WINDOW)
        reach = column[tile * TILE : (tile + 1) * TILE, 0:1]
        inside = (offset >= -reach) & (offset < reach) & (position >= 0) & (position < place_ref[1])
        bias_ref[tile] = jnp.where(inside, 0.0, -1e30)

    first = lane_index(1, LANES) < HEAD

    for pair in range(HEADS // 2):
        lanes = slice(pair * LANES, (pair + 1) * LANES)
        for tile in range(ROWS // TILE):
            rows = slice(tile * TILE, (tile + 1) * TILE)
            window = slice(tile * TILE, tile * TILE + WINDOW)
            queries = q_ref[ROWS + tile * TILE : ROWS + (tile + 1) * TILE, lanes]
            keys = k_ref[window, lanes]
            values = v_ref[window, lanes]
            bias = bias_ref[tile]
            outs = []
            for mine in (first, ~first):
                score = mm_t(jnp.where(mine, queries, jnp.zeros_like(queries)), keys)
                weight = jnp.exp2(score * exponent_scale + bias).astype(bf16)
                outs.append(mm(weight, jnp.where(mine, values, jnp.ones_like(values))))
            total = pltpu.roll(jnp.where(first, outs[1], outs[0]), HEAD, 1)
            mixed = jnp.where(first, outs[0], outs[1]) / total
            mixed_ref[rows, lanes] = mixed
            mixed_low_ref[rows, lanes] = mixed.astype(bf16)
            total_ref[rows, lanes] = total

    near, far = core_halves(place_ref, INNER // 2)
    left, right = mixed_low_ref[:, near], mixed_low_ref[:, far]
    forecast = jnp.zeros((ROWS, LANES), f32)
    for side in range(2):
        columns = slice(side * INNER, (side + 1) * INNER)
        branch = mm(left, out_weights(wa_ref, side)) + mm(right, out_weights(wb_ref, side))
        hidden = latent_ref[:, columns].astype(f32) + pert_ref[:, columns].astype(f32)
        updated = (hidden + branch).astype(bf16)
        forecast = forecast + mm_t(updated, decoder_ref[:, columns])
    forecast_ref[...] = forecast


def score_kernel(forecast_ref, truth_ref, area_ref, out_ref):
    lanes = lane_index(SLOT, LANES)
    area = jnp.where(lanes < VARS, area_ref[...], 0.0)
    truth = truth_ref[...]
    square = smooth_width * smooth_width
    loss = jnp.zeros((SLOT, LANES), f32)
    for member in range(MEMBERS):
        own = forecast_ref[member]
        pull = jnp.zeros((SLOT, LANES), f32)
        spread = jnp.zeros((SLOT, LANES), f32)
        for other in range(MEMBERS):
            if other == member:
                continue
            gap = own - forecast_ref[other]
            power = gap * gap + square
            inverse = lax.rsqrt(power)
            pull = pull + gap * inverse
            spread = spread + power * inverse
        gap = own - truth
        power = gap * gap + square
        inverse = lax.rsqrt(power)
        loss = loss + area * (power * inverse - spread * (0.5 / (MEMBERS - 1)))
        out_ref[member] = (area * (gap * inverse - pull * (1.0 / (MEMBERS - 1)))).astype(bf16)
    total = jnp.sum(jnp.sum(loss, axis=1, keepdims=True), axis=0, keepdims=True)
    total = jnp.broadcast_to(total, (SLOT, LANES))
    high, rest = split(total)
    middle = rest
    low = (total - high.astype(f32) - middle.astype(f32)).astype(bf16)
    for member in range(MEMBERS):
        kept = out_ref[member]
        kept = jnp.where(lanes == VARS, high, kept)
        kept = jnp.where(lanes == VARS + 1, middle, kept)
        out_ref[member] = jnp.where(lanes == VARS + 2, low, kept)


def mixed_gradient(upd_low, place_ref, wa_ref, wb_ref, target_ref):
    for w_ref, lanes in zip((wa_ref, wb_ref), core_halves(place_ref, INNER // 2)):
        target_ref[:, lanes] = mm_t(upd_low[:, :INNER], out_weights(w_ref, 0)) + mm_t(
            upd_low[:, INNER:], out_weights(w_ref, 1)
        )
    return target_ref[...].astype(bf16).astype(f32)


def gradient_operands(scaled, row_dot, g0_ref, g1_ref, rows):
    first = lane_index(1, LANES) < HEAD
    spot = lane_index(ROWS, LANES) % HEAD
    for pair in range(HEADS // 2):
        lanes = slice(pair * LANES, (pair + 1) * LANES)
        high, low = split(-pltpu.roll(row_dot[:, lanes], HEAD, 1))
        zero = jnp.zeros_like(high)
        extra = jnp.where(spot == 0, high, jnp.where(spot == 1, low, zero))
        own = scaled[:, lanes]
        g0_ref[rows, lanes] = jnp.where(first, own, extra)
        g1_ref[rows, lanes] = jnp.where(first, extra, own)


def pick(rows, lanes):
    row = lax.broadcasted_iota(jnp.int32, (rows, lanes), 0)
    lane = lane_index(rows, lanes)
    return row, lane


def upstream_kernel(
    place_ref, pg_ref, decoder_ref, wa_ref, wb_ref, mixed_ref, total_ref, reach_ref,
    upd_ref, scaled_ref, g0_ref, g1_ref, message_ref, loss_ref, grad_ref,
):
    pg = pg_ref[...]
    upd = mm(pg, decoder_ref[...])
    upd_ref[...] = upd
    everything = slice(0, ROWS)
    grad = mixed_gradient(upd.astype(bf16), place_ref, wa_ref, wb_ref, grad_ref)
    total = total_ref[...]
    inverse = 1.0 / total
    row_dot = head_sums(grad * mixed_ref[...], segment_matrix(1.0)) * inverse
    scaled = (grad * inverse).astype(bf16)
    scaled_ref[...] = scaled
    gradient_operands(scaled, row_dot, g0_ref, g1_ref, everything)

    row, lane = pick(INNER, LANES)
    head_row = (row % HEAD == 0)
    chosen = lambda start: jnp.where(head_row & (lane == start + row // HEAD), 1.0, 0.0).astype(bf16)
    high, low = split(total)
    stats = mm(high, chosen(VARS)) + mm(low, chosen(VARS + 8)) + mm(row_dot.astype(bf16), chosen(VARS + 16))
    lanes = lane_index(ROWS, LANES)
    message = jnp.where(lanes < VARS, pg.astype(f32), stats)
    message = jnp.where(lanes == REACH_LANE, column_of(reach_ref).astype(f32), message)
    kept = jnp.where((lanes >= VARS) & (lanes < VARS + 3), pg.astype(f32), 0.0)
    loss = jnp.sum(jnp.sum(kept, axis=1, keepdims=True), axis=0, keepdims=True) * (1.0 / SLOT)
    loss_ref[...] = jnp.broadcast_to(loss, (8, LANES))
    high, middle = split(loss)
    low = (loss - high.astype(f32) - middle.astype(f32)).astype(bf16)
    for lane, part in enumerate((high, middle, low)):
        message = jnp.where(lanes == LOSS_LANE + lane, part.astype(f32), message)
    message_ref[...] = message.astype(bf16)


def pair_kernel(place_ref, own_ref, low_ref, high_ref, out_ref):
    lanes = lane_index(1, LANES)
    even = place_ref[3] == 0
    nearby = jnp.where(even, high_ref[0:16, :].astype(f32), low_ref[0:16, :].astype(f32))[0:1, :]
    nearby = jnp.where((lanes >= LOSS_LANE) & (lanes < LOSS_LANE + 3), nearby, 0.0)
    out_ref[...] = own_ref[...] + jnp.sum(nearby, axis=1, keepdims=True)


def query_kernel(
    place_ref, q_ref, k_ref, v_ref, g0_ref, g1_ref, reach_ref, qgrad_ref, bias_ref,
):
    row_start = place_ref[0]
    column = column_of(reach_ref)
    for tile in range(ROWS // TILE):
        offset = (
            lane_index(TILE, WINDOW)
            - HALF
            - lax.broadcasted_iota(jnp.int32, (TILE, WINDOW), 0)
        )
        position = row_start - HALF + tile * TILE + lane_index(TILE, WINDOW)
        reach = column[tile * TILE : (tile + 1) * TILE, 0:1]
        inside = (offset >= -reach) & (offset < reach) & (position >= 0) & (position < place_ref[1])
        bias_ref[tile] = jnp.where(inside, 0.0, -1e30)
    first = lane_index(1, LANES) < HEAD

    for pair in range(HEADS // 2):
        lanes = slice(pair * LANES, (pair + 1) * LANES)
        for tile in range(ROWS // TILE):
            rows = slice(tile * TILE, (tile + 1) * TILE)
            window = slice(tile * TILE, tile * TILE + WINDOW)
            queries = q_ref[ROWS + tile * TILE : ROWS + (tile + 1) * TILE, lanes]
            keys = k_ref[window, lanes]
            values = v_ref[window, lanes]
            bias = bias_ref[tile]
            grads = []
            for mine, g_ref in ((first, g0_ref), (~first, g1_ref)):
                score = mm_t(jnp.where(mine, queries, jnp.zeros_like(queries)), keys)
                weight = jnp.exp2(score * exponent_scale + bias)
                pull = mm_t(g_ref[rows, lanes], jnp.where(mine, values, jnp.ones_like(values)))
                grads.append(mm((weight * pull).astype(bf16), keys))
            qgrad_ref[rows, lanes] = jnp.where(first, grads[0], grads[1]) * 0.125


def backward_kernel(
    place_ref, low_ref, high_ref, decoder_ref, wa_ref, wb_ref, q_ref, k_ref, v_ref,
    scaled_ref, g0_ref, g1_ref, reach_ref, qgrad_ref, unit_ref, factor_ref,
    qkv_grad_ref,
    all_scaled, all_g0, all_g1, all_reach, bias_ref, grad_ref, kv_ref,
):
    row, lane = pick(LANES, INNER)
    spread = lambda start: row == start + lane // HEAD
    expand_total = jnp.where(spread(VARS) | spread(VARS + 8), 1.0, 0.0).astype(bf16)
    expand_dot = jnp.where(spread(VARS + 16), 1.0, 0.0).astype(bf16)
    middle = slice(ROWS, 2 * ROWS)
    all_scaled[middle, :] = scaled_ref[...]
    all_g0[middle, :] = g0_ref[...]
    all_g1[middle, :] = g1_ref[...]
    all_reach[:, middle] = jnp.broadcast_to(reach_ref[...], (8, ROWS))
    for block, message_ref in ((0, low_ref), (2, high_ref)):
        rows = slice(block * ROWS, (block + 1) * ROWS)
        message = message_ref[...]
        turned = message.astype(f32).T
        all_reach[:, rows] = jnp.broadcast_to(turned[REACH_LANE : REACH_LANE + 1, :], (8, ROWS)).astype(jnp.int32)
        grad = mixed_gradient(
            mm(message, decoder_ref[...]).astype(bf16), place_ref, wa_ref, wb_ref, grad_ref
        )
        total = mm(message, expand_total)
        scaled = (grad / jnp.where(total > 0.0, total, 1.0)).astype(bf16)
        all_scaled[rows, :] = scaled
        gradient_operands(scaled, mm(message, expand_dot), all_g0, all_g1, rows)

    for tile in range(ROWS // TILE):
        offset = (
            HALF
            + lax.broadcasted_iota(jnp.int32, (TILE, WINDOW), 0)
            - lane_index(TILE, WINDOW)
        )
        reach = all_reach[0:1, tile * TILE : tile * TILE + WINDOW]
        bias_ref[tile] = jnp.where((offset >= -reach) & (offset < reach), 0.0, -1e30)
    first = lane_index(1, LANES) < HEAD

    for pair in range(HEADS // 2):
        lanes = slice(pair * LANES, (pair + 1) * LANES)
        value_lanes = slice(INNER + pair * LANES, INNER + (pair + 1) * LANES)
        for tile in range(ROWS // TILE):
            rows = slice(tile * TILE, (tile + 1) * TILE)
            window = slice(tile * TILE, tile * TILE + WINDOW)
            keys = k_ref[ROWS + tile * TILE : ROWS + (tile + 1) * TILE, lanes]
            values = v_ref[ROWS + tile * TILE : ROWS + (tile + 1) * TILE, lanes]
            queries = q_ref[window, lanes]
            scaled = all_scaled[window, lanes]
            bias = bias_ref[tile]
            key_grads = []
            value_grads = []
            for mine, g_ref in ((first, all_g0), (~first, all_g1)):
                score = mm_t(jnp.where(mine, keys, jnp.zeros_like(keys)), queries)
                weight = jnp.exp2(score * exponent_scale + bias)
                pull = mm_t(jnp.where(mine, values, jnp.ones_like(values)), g_ref[window, lanes])
                value_grads.append(mm(weight.astype(bf16), scaled))
                key_grads.append(mm((weight * pull).astype(bf16), queries))
            kv_ref[rows, lanes] = jnp.where(first, key_grads[0], key_grads[1]) * 0.125
            kv_ref[rows, value_lanes] = jnp.where(first, value_grads[0], value_grads[1])

    segments = segment_matrix(1.0 / HEAD)
    for part, grad in ((0, qgrad_ref[...]), (1, kv_ref[:, :INNER])):
        columns = slice(part * INNER, (part + 1) * INNER)
        unit = unit_ref[:, columns]
        along = head_means(grad * unit, segments)
        qkv_grad_ref[:, columns] = (factor_ref[:, columns] * (grad - unit * along)).astype(bf16)
    qkv_grad_ref[:, 2 * INNER :] = kv_ref[:, INNER:].astype(bf16)


def hidden_kernel(
    place_ref, qkv_grad_ref, wa_ref, wb_ref, latent_ref, pert_ref, gain_ref, upd_ref, loss_ref,
    noise_ref, send_ref, normed_grad_ref,
):
    parts = [qkv_grad_ref[:, part * INNER : (part + 1) * INNER] for part in range(3)]
    for w_ref, lanes in zip((wa_ref, wb_ref), core_halves(place_ref, INNER)):
        normed_grad_ref[:, lanes] = (
            mm_t(parts[0], qkv_weights(w_ref, 0))
            + mm_t(parts[1], qkv_weights(w_ref, 1))
            + mm_t(parts[2], qkv_weights(w_ref, 2))
        )
    gain = gain_ref[...].astype(f32)
    for part in range(ROWS // TILE):
        rows = slice(part * TILE, (part + 1) * TILE)
        hidden = latent_ref[rows, :].astype(f32) + pert_ref[rows, :].astype(f32)
        centred = hidden - jnp.mean(hidden, axis=1, keepdims=True)
        inverse = lax.rsqrt(jnp.mean(centred * centred, axis=1, keepdims=True) + norm_epsilon)
        standard = centred * inverse
        grad = normed_grad_ref[rows, :] * gain
        first_term = jnp.mean(grad, axis=1, keepdims=True)
        second_term = standard * jnp.mean(grad * standard, axis=1, keepdims=True)
        result = upd_ref[rows, :] + inverse * (grad - first_term - second_term)
        noise_ref[rows, :] = result
        turned = result.T.astype(bf16)
        for member in range(MEMBERS):
            send_ref[member, :HEAD, rows] = turned[member * HEAD : (member + 1) * HEAD, :]
    loss = jnp.broadcast_to(loss_ref[0:1, 0:1], (16, ROWS))
    high, middle = split(loss)
    low = (loss - high.astype(f32) - middle.astype(f32)).astype(bf16)
    lanes = lane_index(16, ROWS)
    tail = jnp.zeros((16, ROWS), f32)
    for lane, part in enumerate((high, middle, low)):
        tail = jnp.where(lanes == lane, part.astype(f32), tail)
    for member in range(MEMBERS):
        send_ref[member, HEAD:, :] = tail.astype(bf16)


def finish_kernel(scale, received_ref, latent_grad_ref, loss_ref):
    total = received_ref[0].astype(f32)
    for member in range(1, MEMBERS):
        total = total + received_ref[member].astype(f32)
    latent_grad_ref[...] = total[:HEAD]
    loss_ref[...] = jnp.sum(total[HEAD : HEAD + 1, :], axis=1, keepdims=True) * scale


def call(body, outs, scratch, megabytes, cost, *operands, far=()):
    spaces = [
        pltpu.SMEM if o.dtype == jnp.int32 and o.ndim == 1 else pltpu.HBM if i in far else pltpu.VMEM
        for i, o in enumerate(operands)
    ]
    specs = [pl.BlockSpec(memory_space=space) for space in spaces]
    semaphores = [pltpu.SemaphoreType.DMA((len(far),))] if far else []
    result = pl.pallas_call(
        body,
        out_shape=tuple(jax.ShapeDtypeStruct(shape, kind) for shape, kind in outs),
        in_specs=specs,
        out_specs=tuple(pl.BlockSpec(memory_space=pltpu.VMEM) for _ in outs),
        scratch_shapes=[pltpu.VMEM(shape, kind) for shape, kind in scratch] + semaphores,
        compiler_params=pltpu.CompilerParams(vmem_limit_bytes=megabytes * 1024 * 1024),
        cost_estimate=pl.CostEstimate(flops=cost, bytes_accessed=4_000_000, transcendentals=0),
    )(*operands)
    return result


def both_ways(block):
    count = lax.axis_size(NODE)
    low = lax.ppermute(block, NODE, [(i, i + 1) for i in range(count - 1)])
    high = lax.ppermute(block, NODE, [(i + 1, i) for i in range(count - 1)])
    return low, high


def flat(y, xl, c, z, xh):
    return (((y * 2 + xl) * 2 + c) * 16 + z) * 2 + xh


def rank(y, xl, c):
    return c * 8 + y * 2 + xl


def members():
    return [(y, xl, c) for y in range(4) for xl in range(2) for c in range(2)]


def weight_route():
    by_rank = {rank(*member): member for member in members()}
    pairs = []
    for member in members():
        for z in range(16):
            for xh in range(2):
                source = flat(*by_rank[z], rank(*member), xh)
                pairs.append((source, flat(*member, z, xh)))
    return pairs


def loss_route():
    pairs = []
    for shift, member in enumerate(members()):
        for z in range(16):
            for xh in range(2):
                pairs.append((flat(*member, z, xh), flat(*member, (z + shift) % 16, xh)))
    return pairs


def shards(
    latent,
    member_perturbations,
    layer_norm_gain,
    query_key_value_weight,
    output_weight_matrix,
    decoder_weight_matrix,
    observed_truth,
    region_mask,
    node_window_halfspan,
):
    pert = member_perturbations[0]
    node_total = ROWS * lax.axis_size(NODE)
    member = lax.axis_index(MEMBER)
    place = jnp.stack([lax.axis_index(NODE) * ROWS, jnp.int32(node_total), lax.axis_index("c"), lax.axis_index("xh")]).astype(jnp.int32)

    packed = jnp.concatenate(
        [
            query_key_value_weight,
            jnp.concatenate([output_weight_matrix[:, :INNER], output_weight_matrix[:, INNER:]], axis=0),
        ],
        axis=1,
    )
    with jax.named_scope("weights_over_node"):
        mine = lax.ppermute(packed, EVERY, weight_route())
    latent_copies = jnp.broadcast_to(latent.T[None], (MEMBERS, HEAD, ROWS))
    with jax.named_scope("latent_over_member"):
        latent_turned = lax.all_to_all(latent_copies, MEMBER, 0, 0, tiled=True).reshape(WIDTH, ROWS)
    with jax.named_scope("layer_norm"):
        normed, latent_own = call(
            norm_kernel,
            [((ROWS, WIDTH), bf16), ((ROWS, WIDTH), bf16)],
            [],
            8,
            1_000_000_000,
            latent_turned, pert, layer_norm_gain[None],
        )
    (mine, normed, decoder_weight_matrix, observed_truth, region_mask, gain, reach_row, place) = (
        lax.optimization_barrier(
            (mine, normed, decoder_weight_matrix, observed_truth, region_mask, layer_norm_gain[None],
             node_window_halfspan[None], place)
        )
    )
    decoder = jnp.pad(decoder_weight_matrix, ((0, LANES - VARS), (0, 0)))
    truth = lax.dynamic_slice_in_dim(observed_truth, member * SLOT, SLOT, 1)
    truth = jnp.pad(truth.T, ((0, 0), (0, LANES - VARS)))
    mask = lax.dynamic_slice_in_dim(region_mask, member * SLOT, SLOT, 0)
    area = (1.0 - (1.0 - region_share) * mask.astype(f32))[:, None]
    area = jnp.broadcast_to(area, (SLOT, LANES))
    with jax.named_scope("normed_halo"):
        normed_low, normed_high = both_ways(normed)
    with jax.named_scope("weights_over_x"):
        row = lax.all_to_all(jnp.broadcast_to(mine[None], (4,) + mine.shape), ("xl", "xh"), 0, 0, tiled=True)
        row = row.reshape(128, PACKED)
    with jax.named_scope("weights_over_y"):
        wa = lax.all_to_all(jnp.broadcast_to(row[None], (4,) + row.shape), "y", 0, 0, tiled=True)
        wa = wa.reshape(16, 32, PACKED)
    wa, normed_low, normed_high, decoder, truth, area, gain, reach_row, place = lax.optimization_barrier(
        (wa, normed_low, normed_high, decoder, truth, area, gain, reach_row, place)
    )
    with jax.named_scope("normed_rows"):
        normed_all = jnp.concatenate([normed_low, normed, normed_high], axis=0)
    with jax.named_scope("weights_over_core"):
        wb = lax.ppermute(wa, "c", [(0, 1), (1, 0)])
    with jax.named_scope("forward"):
        q, k, v, unit, factor, mixed, total, forecast = call(
            forward_kernel,
            [((EXT, INNER), bf16)] * 3
            + [((ROWS, WIDTH), f32)] * 2
            + [((ROWS, INNER), f32)] * 2
            + [((ROWS, LANES), f32)],
            [((2, TILE, WINDOW), f32), ((ROWS, INNER), bf16)],
            40,
            4_000_000_000,
            place, normed_all, wa, wb, latent_own, pert, reach_row, decoder,
        )
    with jax.named_scope("forecasts_over_member"):
        forecasts = lax.all_to_all(
            forecast.reshape(MEMBERS, SLOT, LANES), MEMBER, 0, 0, tiled=True
        )
    with jax.named_scope("score"):
        (pred_grads,) = call(
            score_kernel, [((MEMBERS, SLOT, LANES), bf16)], [], 8, 10_000_000, forecasts, truth, area
        )
    with jax.named_scope("gradients_over_member"):
        pred_grad = lax.all_to_all(pred_grads, MEMBER, 0, 0, tiled=True).reshape(ROWS, LANES)
    with jax.named_scope("upstream"):
        upd, scaled, g0, g1, message, loss_part = call(
            upstream_kernel,
            [((ROWS, WIDTH), f32)] + [((ROWS, INNER), bf16)] * 3 + [((ROWS, LANES), bf16), ((8, LANES), f32)],
            [((ROWS, INNER), f32)],
            16,
            500_000_000,
            place, pred_grad, decoder, wa, wb, mixed, total, reach_row,
        )
    with jax.named_scope("gradient_halo"):
        message_low, message_high = both_ways(message)
    with jax.named_scope("query_gradients"):
        (qgrad,) = call(
            query_kernel,
            [((ROWS, INNER), f32)],
            [((2, TILE, WINDOW), f32)],
            12,
            4_000_000_000,
            place, q, k, v, g0, g1, reach_row,
        )
    with jax.named_scope("loss_over_node"):
        (loss_part,) = call(
            pair_kernel, [((8, LANES), f32)], [], 4, 10_000, place, loss_part, message_low, message_high
        )
        loss_part = lax.ppermute(loss_part, EVERY, loss_route())
    with jax.named_scope("backward"):
        (qkv_grad,) = call(
            backward_kernel,
            [((ROWS, 3 * INNER), bf16)],
            [((EXT, INNER), bf16)] * 3
            + [((8, EXT), jnp.int32)]
            + [((2, TILE, WINDOW), f32), ((ROWS, INNER), f32), ((ROWS, WIDTH), f32)],
            24,
            4_000_000_000,
            place, message_low, message_high, decoder, wa, wb, q, k, v, scaled, g0, g1, reach_row,
            qgrad, unit, factor,
        )
    with jax.named_scope("hidden_gradient"):
        noise, send = call(
            hidden_kernel,
            [((ROWS, WIDTH), f32), ((MEMBERS, HEAD + 16, ROWS), bf16)],
            [((ROWS, WIDTH), f32)],
            16,
            1_000_000_000,
            place, qkv_grad, wa, wb, latent_own, pert, gain, upd, loss_part,
        )
    with jax.named_scope("latent_gradient_over_member"):
        received = lax.all_to_all(send, MEMBER, 0, 0, tiled=True)
    with jax.named_scope("finish"):
        latent_grad, loss = call(
            functools.partial(finish_kernel, 1.0 / (MEMBERS * node_total * VARS)),
            [((HEAD, ROWS), f32), ((1, 1), f32)], [], 8, 10_000_000, received,
        )
    return (loss.reshape(()), latent_grad.T, noise[None])


def solution(mesh):
    fine = Mesh(mesh.devices.reshape(4, 2, 2, 16, 2), EVERY)
    placed = (
        P(NODE, MEMBER),
        P(MEMBER, NODE, None),
        P(),
        P(NODE, None),
        P(NODE, None),
        P(),
        P(None, NODE),
        P(NODE),
        P(NODE),
    )
    return jax.shard_map(
        shards,
        mesh=fine,
        in_specs=placed,
        out_specs=(P(), P(NODE, MEMBER), P(MEMBER, NODE, None)),
        check_vma=False,
    )
```

```python
import functools
import math

import jax
import jax.numpy as jnp
from jax import lax
from jax.experimental import pallas as pl
from jax.experimental.pallas import tpu as pltpu
from jax.sharding import Mesh, PartitionSpec as P

HEADS = 8
HEAD = 64
INNER = 512
ROWS = 256
HALF = 256
EXT = ROWS + 2 * HALF
WIDTH = 1024
VARS = 98
LANES = 128
MEMBERS = 16
SLOT = ROWS // MEMBERS
TILE = 256
WINDOW = TILE + 2 * HALF
LOSS_LANE = 122
REACH_LANE = 125
BLOCK = 256
PACKED = 2048

norm_epsilon = 1e-05
head_epsilon = 1e-06
smooth_width = 0.1
region_share = 0.25
exponent_scale = math.log2(math.e) / 8.0

MEMBER = ("y", "xl", "c")
NODE = ("z", "xh")
EVERY = MEMBER + NODE

bf16 = jnp.bfloat16
f32 = jnp.float32


def mm(left, right):
    return lax.dot_general(left, right, (((1,), (0,)), ((), ())), preferred_element_type=f32)


def mm_t(left, right):
    return lax.dot_general(left, right, (((1,), (1,)), ((), ())), preferred_element_type=f32)


def split(value):
    high = value.astype(bf16)
    return high, (value - high.astype(f32)).astype(bf16)


def segment_matrix(scale):
    rows = lax.broadcasted_iota(jnp.int32, (BLOCK, BLOCK), 0) // HEAD
    columns = lax.broadcasted_iota(jnp.int32, (BLOCK, BLOCK), 1) // HEAD
    return jnp.where(rows == columns, scale, 0.0).astype(bf16)


def head_sums(value, segments):
    high, low = split(value)
    parts = []
    for start in range(0, INNER, BLOCK):
        lanes = slice(start, start + BLOCK)
        parts.append(mm(high[:, lanes], segments) + mm(low[:, lanes], segments))
    return jnp.concatenate(parts, axis=1)


def head_means(value, segments):
    rounded = value.astype(bf16)
    return jnp.concatenate(
        [mm(rounded[:, start : start + BLOCK], segments) for start in range(0, INNER, BLOCK)], axis=1
    )


def lane_index(rows, lanes):
    return lax.broadcasted_iota(jnp.int32, (rows, lanes), 1)


def copies_kernel(block_ref, out_ref):
    out_ref[0] = block_ref[...]


def copies(block, count):
    return pl.pallas_call(
        copies_kernel,
        grid=(count,),
        out_shape=jax.ShapeDtypeStruct((count,) + block.shape, block.dtype),
        in_specs=[pl.BlockSpec(block.shape, lambda i: (0, 0))],
        out_specs=pl.BlockSpec((1,) + block.shape, lambda i: (i, 0, 0)),
        compiler_params=pltpu.CompilerParams(vmem_limit_bytes=8 * 1024 * 1024),
        cost_estimate=pl.CostEstimate(flops=0, bytes_accessed=2 * count * block.size, transcendentals=0),
    )(block)


def norm_kernel(lat_ref, pert_ref, gain_ref, normed_ref, latent_ref):
    gain = gain_ref[...].astype(f32)
    for part in range(ROWS // TILE):
        rows = slice(part * TILE, (part + 1) * TILE)
        lat = lat_ref[:, rows].astype(f32).T
        latent_ref[rows, :] = lat.astype(bf16)
        hidden = lat + pert_ref[rows, :].astype(f32)
        centred = hidden - jnp.mean(hidden, axis=1, keepdims=True)
        inverse = lax.rsqrt(jnp.mean(centred * centred, axis=1, keepdims=True) + norm_epsilon)
        normed_ref[rows, :] = (centred * inverse * gain).astype(bf16)


def out_weights(w_ref, side):
    rows = slice(side * 16, side * 16 + 16)
    return w_ref[:, rows, 3 * INNER :].reshape(INNER // 2, INNER)


def qkv_weights(w_ref, part):
    return w_ref[:, :, part * INNER : (part + 1) * INNER].reshape(INNER, INNER)


def core_halves(place_ref, size):
    core = place_ref[2]
    return (
        pl.ds(pl.multiple_of(core * size, size), size),
        pl.ds(pl.multiple_of((1 - core) * size, size), size),
    )


def column_of(row_ref):
    row = jnp.broadcast_to(row_ref[...].astype(f32), (LANES, ROWS))
    return row.T.astype(jnp.int32)


def forward_kernel(
    place_ref, normed_ref, wa_ref, wb_ref, latent_ref, pert_ref, reach_ref, decoder_ref,
    q_ref, k_ref, v_ref, unit_ref, factor_ref, mixed_ref, total_ref, forecast_ref,
    bias_ref, mixed_low_ref,
):
    row_start = place_ref[0]
    segments = segment_matrix(1.0 / HEAD)
    near, far = core_halves(place_ref, INNER)
    for block in range(3):
        rows = slice(block * ROWS, (block + 1) * ROWS)
        left, right = normed_ref[rows, near], normed_ref[rows, far]
        together = mm(left, wa_ref[:, :, : 3 * INNER].reshape(INNER, 3 * INNER)) + mm(
            right, wb_ref[:, :, : 3 * INNER].reshape(INNER, 3 * INNER)
        )
        for part, out_ref in enumerate((q_ref, k_ref, v_ref)):
            projected = together[:, part * INNER : (part + 1) * INNER]
            if part < 2:
                factor = lax.rsqrt(head_means(projected * projected, segments) + head_epsilon)
                unit = projected * factor
                if block == 1:
                    unit_ref[:, part * INNER : (part + 1) * INNER] = unit
                    factor_ref[:, part * INNER : (part + 1) * INNER] = factor
                projected = unit
            out_ref[rows, :] = projected.astype(bf16)

    column = column_of(reach_ref)
    for tile in range(ROWS // TILE):
        offset = (
            lane_index(TILE, WINDOW)
            - HALF
            - lax.broadcasted_iota(jnp.int32, (TILE, WINDOW), 0)
        )
        position = row_start - HALF + tile * TILE + lane_index(TILE, WINDOW)
        reach = column[tile * TILE : (tile + 1) * TILE, 0:1]
        inside = (offset >= -reach) & (offset < reach) & (position >= 0) & (position < place_ref[1])
        bias_ref[tile] = jnp.where(inside, 0.0, -1e30)

    first = lane_index(1, LANES) < HEAD

    for pair in range(HEADS // 2):
        lanes = slice(pair * LANES, (pair + 1) * LANES)
        for tile in range(ROWS // TILE):
            rows = slice(tile * TILE, (tile + 1) * TILE)
            window = slice(tile * TILE, tile * TILE + WINDOW)
            queries = q_ref[ROWS + tile * TILE : ROWS + (tile + 1) * TILE, lanes]
            keys = k_ref[window, lanes]
            values = v_ref[window, lanes]
            bias = bias_ref[tile]
            outs = []
            for mine in (first, ~first):
                score = mm_t(jnp.where(mine, queries, jnp.zeros_like(queries)), keys)
                weight = jnp.exp2(score * exponent_scale + bias).astype(bf16)
                outs.append(mm(weight, jnp.where(mine, values, jnp.ones_like(values))))
            total = pltpu.roll(jnp.where(first, outs[1], outs[0]), HEAD, 1)
            mixed = jnp.where(first, outs[0], outs[1]) / total
            mixed_ref[rows, lanes] = mixed
            mixed_low_ref[rows, lanes] = mixed.astype(bf16)
            total_ref[rows, lanes] = total

    near, far = core_halves(place_ref, INNER // 2)
    left, right = mixed_low_ref[:, near], mixed_low_ref[:, far]
    forecast = jnp.zeros((ROWS, LANES), f32)
    for side in range(2):
        columns = slice(side * INNER, (side + 1) * INNER)
        branch = mm(left, out_weights(wa_ref, side)) + mm(right, out_weights(wb_ref, side))
        hidden = latent_ref[:, columns].astype(f32) + pert_ref[:, columns].astype(f32)
        updated = (hidden + branch).astype(bf16)
        forecast = forecast + mm_t(updated, decoder_ref[:, columns])
    forecast_ref[...] = forecast


def score_kernel(forecast_ref, truth_ref, area_ref, out_ref):
    lanes = lane_index(SLOT, LANES)
    area = jnp.where(lanes < VARS, area_ref[...], 0.0)
    truth = truth_ref[...]
    square = smooth_width * smooth_width
    loss = jnp.zeros((SLOT, LANES), f32)
    for member in range(MEMBERS):
        own = forecast_ref[member]
        pull = jnp.zeros((SLOT, LANES), f32)
        spread = jnp.zeros((SLOT, LANES), f32)
        for other in range(MEMBERS):
            if other == member:
                continue
            gap = own - forecast_ref[other]
            power = gap * gap + square
            inverse = lax.rsqrt(power)
            pull = pull + gap * inverse
            spread = spread + power * inverse
        gap = own - truth
        power = gap * gap + square
        inverse = lax.rsqrt(power)
        loss = loss + area * (power * inverse - spread * (0.5 / (MEMBERS - 1)))
        out_ref[member] = (area * (gap * inverse - pull * (1.0 / (MEMBERS - 1)))).astype(bf16)
    total = jnp.sum(jnp.sum(loss, axis=1, keepdims=True), axis=0, keepdims=True)
    total = jnp.broadcast_to(total, (SLOT, LANES))
    high, rest = split(total)
    middle = rest
    low = (total - high.astype(f32) - middle.astype(f32)).astype(bf16)
    for member in range(MEMBERS):
        kept = out_ref[member]
        kept = jnp.where(lanes == VARS, high, kept)
        kept = jnp.where(lanes == VARS + 1, middle, kept)
        out_ref[member] = jnp.where(lanes == VARS + 2, low, kept)


def mixed_gradient(upd_low, place_ref, wa_ref, wb_ref, target_ref):
    for w_ref, lanes in zip((wa_ref, wb_ref), core_halves(place_ref, INNER // 2)):
        target_ref[:, lanes] = mm_t(upd_low[:, :INNER], out_weights(w_ref, 0)) + mm_t(
            upd_low[:, INNER:], out_weights(w_ref, 1)
        )
    return target_ref[...].astype(bf16).astype(f32)


def gradient_operands(scaled, row_dot, g0_ref, g1_ref, rows):
    first = lane_index(1, LANES) < HEAD
    spot = lane_index(ROWS, LANES) % HEAD
    for pair in range(HEADS // 2):
        lanes = slice(pair * LANES, (pair + 1) * LANES)
        high, low = split(-pltpu.roll(row_dot[:, lanes], HEAD, 1))
        zero = jnp.zeros_like(high)
        extra = jnp.where(spot == 0, high, jnp.where(spot == 1, low, zero))
        own = scaled[:, lanes]
        g0_ref[rows, lanes] = jnp.where(first, own, extra)
        g1_ref[rows, lanes] = jnp.where(first, extra, own)


def pick(rows, lanes):
    row = lax.broadcasted_iota(jnp.int32, (rows, lanes), 0)
    lane = lane_index(rows, lanes)
    return row, lane


def upstream_kernel(
    place_ref, pg_ref, decoder_ref, wa_ref, wb_ref, mixed_ref, total_ref, reach_ref,
    upd_ref, scaled_ref, g0_ref, g1_ref, message_ref, loss_ref, grad_ref,
):
    pg = pg_ref[...]
    upd = mm(pg, decoder_ref[...])
    upd_ref[...] = upd
    everything = slice(0, ROWS)
    grad = mixed_gradient(upd.astype(bf16), place_ref, wa_ref, wb_ref, grad_ref)
    total = total_ref[...]
    inverse = 1.0 / total
    row_dot = head_sums(grad * mixed_ref[...], segment_matrix(1.0)) * inverse
    scaled = (grad * inverse).astype(bf16)
    scaled_ref[...] = scaled
    gradient_operands(scaled, row_dot, g0_ref, g1_ref, everything)

    row, lane = pick(INNER, LANES)
    head_row = (row % HEAD == 0)
    chosen = lambda start: jnp.where(head_row & (lane == start + row // HEAD), 1.0, 0.0).astype(bf16)
    high, low = split(total)
    stats = mm(high, chosen(VARS)) + mm(low, chosen(VARS + 8)) + mm(row_dot.astype(bf16), chosen(VARS + 16))
    lanes = lane_index(ROWS, LANES)
    message = jnp.where(lanes < VARS, pg.astype(f32), stats)
    message = jnp.where(lanes == REACH_LANE, column_of(reach_ref).astype(f32), message)
    kept = jnp.where((lanes >= VARS) & (lanes < VARS + 3), pg.astype(f32), 0.0)
    loss = jnp.sum(jnp.sum(kept, axis=1, keepdims=True), axis=0, keepdims=True) * (1.0 / SLOT)
    loss_ref[...] = jnp.broadcast_to(loss, (8, LANES))
    high, middle = split(loss)
    low = (loss - high.astype(f32) - middle.astype(f32)).astype(bf16)
    for lane, part in enumerate((high, middle, low)):
        message = jnp.where(lanes == LOSS_LANE + lane, part.astype(f32), message)
    message_ref[...] = message.astype(bf16)


def pair_kernel(place_ref, own_ref, low_ref, high_ref, out_ref):
    lanes = lane_index(1, LANES)
    even = place_ref[3] == 0
    nearby = jnp.where(even, high_ref[0:16, :].astype(f32), low_ref[0:16, :].astype(f32))[0:1, :]
    nearby = jnp.where((lanes >= LOSS_LANE) & (lanes < LOSS_LANE + 3), nearby, 0.0)
    out_ref[...] = own_ref[...] + jnp.sum(nearby, axis=1, keepdims=True)


def query_kernel(
    place_ref, q_ref, k_ref, v_ref, g0_ref, g1_ref, reach_ref, qgrad_ref, bias_ref,
):
    row_start = place_ref[0]
    column = column_of(reach_ref)
    for tile in range(ROWS // TILE):
        offset = (
            lane_index(TILE, WINDOW)
            - HALF
            - lax.broadcasted_iota(jnp.int32, (TILE, WINDOW), 0)
        )
        position = row_start - HALF + tile * TILE + lane_index(TILE, WINDOW)
        reach = column[tile * TILE : (tile + 1) * TILE, 0:1]
        inside = (offset >= -reach) & (offset < reach) & (position >= 0) & (position < place_ref[1])
        bias_ref[tile] = jnp.where(inside, 0.0, -1e30)
    first = lane_index(1, LANES) < HEAD

    for pair in range(HEADS // 2):
        lanes = slice(pair * LANES, (pair + 1) * LANES)
        for tile in range(ROWS // TILE):
            rows = slice(tile * TILE, (tile + 1) * TILE)
            window = slice(tile * TILE, tile * TILE + WINDOW)
            queries = q_ref[ROWS + tile * TILE : ROWS + (tile + 1) * TILE, lanes]
            keys = k_ref[window, lanes]
            values = v_ref[window, lanes]
            bias = bias_ref[tile]
            grads = []
            for mine, g_ref in ((first, g0_ref), (~first, g1_ref)):
                score = mm_t(jnp.where(mine, queries, jnp.zeros_like(queries)), keys)
                weight = jnp.exp2(score * exponent_scale + bias)
                pull = mm_t(g_ref[rows, lanes], jnp.where(mine, values, jnp.ones_like(values)))
                grads.append(mm((weight * pull).astype(bf16), keys))
            qgrad_ref[rows, lanes] = jnp.where(first, grads[0], grads[1]) * 0.125


def backward_kernel(
    place_ref, low_ref, high_ref, decoder_ref, wa_ref, wb_ref, q_ref, k_ref, v_ref,
    scaled_ref, g0_ref, g1_ref, reach_ref, qgrad_ref, unit_ref, factor_ref,
    qkv_grad_ref,
    all_scaled, all_g0, all_g1, all_reach, bias_ref, grad_ref, kv_ref,
):
    row, lane = pick(LANES, INNER)
    spread = lambda start: row == start + lane // HEAD
    expand_total = jnp.where(spread(VARS) | spread(VARS + 8), 1.0, 0.0).astype(bf16)
    expand_dot = jnp.where(spread(VARS + 16), 1.0, 0.0).astype(bf16)
    middle = slice(ROWS, 2 * ROWS)
    all_scaled[middle, :] = scaled_ref[...]
    all_g0[middle, :] = g0_ref[...]
    all_g1[middle, :] = g1_ref[...]
    all_reach[:, middle] = jnp.broadcast_to(reach_ref[...], (8, ROWS))
    for block, message_ref in ((0, low_ref), (2, high_ref)):
        rows = slice(block * ROWS, (block + 1) * ROWS)
        message = message_ref[...]
        turned = message.astype(f32).T
        all_reach[:, rows] = jnp.broadcast_to(turned[REACH_LANE : REACH_LANE + 1, :], (8, ROWS)).astype(jnp.int32)
        grad = mixed_gradient(
            mm(message, decoder_ref[...]).astype(bf16), place_ref, wa_ref, wb_ref, grad_ref
        )
        total = mm(message, expand_total)
        scaled = (grad / jnp.where(total > 0.0, total, 1.0)).astype(bf16)
        all_scaled[rows, :] = scaled
        gradient_operands(scaled, mm(message, expand_dot), all_g0, all_g1, rows)

    for tile in range(ROWS // TILE):
        offset = (
            HALF
            + lax.broadcasted_iota(jnp.int32, (TILE, WINDOW), 0)
            - lane_index(TILE, WINDOW)
        )
        reach = all_reach[0:1, tile * TILE : tile * TILE + WINDOW]
        bias_ref[tile] = jnp.where((offset >= -reach) & (offset < reach), 0.0, -1e30)
    first = lane_index(1, LANES) < HEAD

    for pair in range(HEADS // 2):
        lanes = slice(pair * LANES, (pair + 1) * LANES)
        value_lanes = slice(INNER + pair * LANES, INNER + (pair + 1) * LANES)
        for tile in range(ROWS // TILE):
            rows = slice(tile * TILE, (tile + 1) * TILE)
            window = slice(tile * TILE, tile * TILE + WINDOW)
            keys = k_ref[ROWS + tile * TILE : ROWS + (tile + 1) * TILE, lanes]
            values = v_ref[ROWS + tile * TILE : ROWS + (tile + 1) * TILE, lanes]
            queries = q_ref[window, lanes]
            scaled = all_scaled[window, lanes]
            bias = bias_ref[tile]
            key_grads = []
            value_grads = []
            for mine, g_ref in ((first, all_g0), (~first, all_g1)):
                score = mm_t(jnp.where(mine, keys, jnp.zeros_like(keys)), queries)
                weight = jnp.exp2(score * exponent_scale + bias)
                pull = mm_t(jnp.where(mine, values, jnp.ones_like(values)), g_ref[window, lanes])
                value_grads.append(mm(weight.astype(bf16), scaled))
                key_grads.append(mm((weight * pull).astype(bf16), queries))
            kv_ref[rows, lanes] = jnp.where(first, key_grads[0], key_grads[1]) * 0.125
            kv_ref[rows, value_lanes] = jnp.where(first, value_grads[0], value_grads[1])

    segments = segment_matrix(1.0 / HEAD)
    for part, grad in ((0, qgrad_ref[...]), (1, kv_ref[:, :INNER])):
        columns = slice(part * INNER, (part + 1) * INNER)
        unit = unit_ref[:, columns]
        along = head_means(grad * unit, segments)
        qkv_grad_ref[:, columns] = (factor_ref[:, columns] * (grad - unit * along)).astype(bf16)
    qkv_grad_ref[:, 2 * INNER :] = kv_ref[:, INNER:].astype(bf16)


def hidden_kernel(
    place_ref, qkv_grad_ref, wa_ref, wb_ref, latent_ref, pert_ref, gain_ref, upd_ref, loss_ref,
    noise_ref, send_ref, normed_grad_ref,
):
    parts = [qkv_grad_ref[:, part * INNER : (part + 1) * INNER] for part in range(3)]
    for w_ref, lanes in zip((wa_ref, wb_ref), core_halves(place_ref, INNER)):
        normed_grad_ref[:, lanes] = (
            mm_t(parts[0], qkv_weights(w_ref, 0))
            + mm_t(parts[1], qkv_weights(w_ref, 1))
            + mm_t(parts[2], qkv_weights(w_ref, 2))
        )
    gain = gain_ref[...].astype(f32)
    for part in range(ROWS // TILE):
        rows = slice(part * TILE, (part + 1) * TILE)
        hidden = latent_ref[rows, :].astype(f32) + pert_ref[rows, :].astype(f32)
        centred = hidden - jnp.mean(hidden, axis=1, keepdims=True)
        inverse = lax.rsqrt(jnp.mean(centred * centred, axis=1, keepdims=True) + norm_epsilon)
        standard = centred * inverse
        grad = normed_grad_ref[rows, :] * gain
        first_term = jnp.mean(grad, axis=1, keepdims=True)
        second_term = standard * jnp.mean(grad * standard, axis=1, keepdims=True)
        result = upd_ref[rows, :] + inverse * (grad - first_term - second_term)
        noise_ref[rows, :] = result
        turned = result.T.astype(bf16)
        for member in range(MEMBERS):
            send_ref[member, :HEAD, rows] = turned[member * HEAD : (member + 1) * HEAD, :]
    loss = jnp.broadcast_to(loss_ref[0:1, 0:1], (16, ROWS))
    high, middle = split(loss)
    low = (loss - high.astype(f32) - middle.astype(f32)).astype(bf16)
    lanes = lane_index(16, ROWS)
    tail = jnp.zeros((16, ROWS), f32)
    for lane, part in enumerate((high, middle, low)):
        tail = jnp.where(lanes == lane, part.astype(f32), tail)
    for member in range(MEMBERS):
        send_ref[member, HEAD:, :] = tail.astype(bf16)


def finish_kernel(scale, received_ref, latent_grad_ref, loss_ref):
    total = received_ref[0].astype(f32)
    for member in range(1, MEMBERS):
        total = total + received_ref[member].astype(f32)
    latent_grad_ref[...] = total[:HEAD]
    loss_ref[...] = jnp.sum(total[HEAD : HEAD + 1, :], axis=1, keepdims=True) * scale


def call(body, outs, scratch, megabytes, cost, *operands, far=()):
    spaces = [
        pltpu.SMEM if o.dtype == jnp.int32 and o.ndim == 1 else pltpu.HBM if i in far else pltpu.VMEM
        for i, o in enumerate(operands)
    ]
    specs = [pl.BlockSpec(memory_space=space) for space in spaces]
    semaphores = [pltpu.SemaphoreType.DMA((len(far),))] if far else []
    result = pl.pallas_call(
        body,
        out_shape=tuple(jax.ShapeDtypeStruct(shape, kind) for shape, kind in outs),
        in_specs=specs,
        out_specs=tuple(pl.BlockSpec(memory_space=pltpu.VMEM) for _ in outs),
        scratch_shapes=[pltpu.VMEM(shape, kind) for shape, kind in scratch] + semaphores,
        compiler_params=pltpu.CompilerParams(vmem_limit_bytes=megabytes * 1024 * 1024),
        cost_estimate=pl.CostEstimate(flops=cost, bytes_accessed=4_000_000, transcendentals=0),
    )(*operands)
    return result


def both_ways(block):
    count = lax.axis_size(NODE)
    low = lax.ppermute(block, NODE, [(i, i + 1) for i in range(count - 1)])
    high = lax.ppermute(block, NODE, [(i + 1, i) for i in range(count - 1)])
    return low, high


def flat(y, xl, c, z, xh):
    return (((y * 2 + xl) * 2 + c) * 16 + z) * 2 + xh


def rank(y, xl, c):
    return c * 8 + y * 2 + xl


def members():
    return [(y, xl, c) for y in range(4) for xl in range(2) for c in range(2)]


def weight_route():
    by_rank = {rank(*member): member for member in members()}
    pairs = []
    for member in members():
        for z in range(16):
            for xh in range(2):
                source = flat(*by_rank[z], rank(*member), xh)
                pairs.append((source, flat(*member, z, xh)))
    return pairs


def loss_route():
    pairs = []
    for shift, member in enumerate(members()):
        for z in range(16):
            for xh in range(2):
                pairs.append((flat(*member, z, xh), flat(*member, (z + shift) % 16, xh)))
    return pairs


def shards(
    latent,
    member_perturbations,
    layer_norm_gain,
    query_key_value_weight,
    output_weight_matrix,
    decoder_weight_matrix,
    observed_truth,
    region_mask,
    node_window_halfspan,
):
    pert = member_perturbations[0]
    node_total = ROWS * lax.axis_size(NODE)
    member = lax.axis_index(MEMBER)
    place = jnp.stack([lax.axis_index(NODE) * ROWS, jnp.int32(node_total), lax.axis_index("c"), lax.axis_index("xh")]).astype(jnp.int32)

    packed = jnp.concatenate(
        [
            query_key_value_weight,
            jnp.concatenate([output_weight_matrix[:, :INNER], output_weight_matrix[:, INNER:]], axis=0),
        ],
        axis=1,
    )
    with jax.named_scope("weights_over_node"):
        mine = lax.ppermute(packed, EVERY, weight_route())
    latent_copies = jnp.broadcast_to(latent.T[None], (MEMBERS, HEAD, ROWS))
    with jax.named_scope("latent_over_member"):
        latent_turned = lax.all_to_all(latent_copies, MEMBER, 0, 0, tiled=True).reshape(WIDTH, ROWS)
    with jax.named_scope("layer_norm"):
        normed, latent_own = call(
            norm_kernel,
            [((ROWS, WIDTH), bf16), ((ROWS, WIDTH), bf16)],
            [],
            8,
            1_000_000_000,
            latent_turned, pert, layer_norm_gain[None],
        )
    (mine, normed, decoder_weight_matrix, observed_truth, region_mask, gain, reach_row, place) = (
        lax.optimization_barrier(
            (mine, normed, decoder_weight_matrix, observed_truth, region_mask, layer_norm_gain[None],
             node_window_halfspan[None], place)
        )
    )
    decoder = jnp.pad(decoder_weight_matrix, ((0, LANES - VARS), (0, 0)))
    truth = lax.dynamic_slice_in_dim(observed_truth, member * SLOT, SLOT, 1)
    truth = jnp.pad(truth.T, ((0, 0), (0, LANES - VARS)))
    mask = lax.dynamic_slice_in_dim(region_mask, member * SLOT, SLOT, 0)
    area = (1.0 - (1.0 - region_share) * mask.astype(f32))[:, None]
    area = jnp.broadcast_to(area, (SLOT, LANES))
    with jax.named_scope("normed_halo"):
        normed_low, normed_high = both_ways(normed)
    with jax.named_scope("weights_over_x"):
        row = lax.all_to_all(jnp.broadcast_to(mine[None], (4,) + mine.shape), ("xl", "xh"), 0, 0, tiled=True)
        row = row.reshape(128, PACKED)
    with jax.named_scope("weights_over_y"):
        wa = lax.all_to_all(copies(row, 4), "y", 0, 0, tiled=True)
        wa = wa.reshape(16, 32, PACKED)
    wa, normed_low, normed_high, decoder, truth, area, gain, reach_row, place = lax.optimization_barrier(
        (wa, normed_low, normed_high, decoder, truth, area, gain, reach_row, place)
    )
    with jax.named_scope("normed_rows"):
        normed_all = jnp.concatenate([normed_low, normed, normed_high], axis=0)
    with jax.named_scope("weights_over_core"):
        wb = lax.ppermute(wa, "c", [(0, 1), (1, 0)])
    with jax.named_scope("forward"):
        q, k, v, unit, factor, mixed, total, forecast = call(
            forward_kernel,
            [((EXT, INNER), bf16)] * 3
            + [((ROWS, WIDTH), f32)] * 2
            + [((ROWS, INNER), f32)] * 2
            + [((ROWS, LANES), f32)],
            [((2, TILE, WINDOW), f32), ((ROWS, INNER), bf16)],
            40,
            4_000_000_000,
            place, normed_all, wa, wb, latent_own, pert, reach_row, decoder,
        )
    with jax.named_scope("forecasts_over_member"):
        forecasts = lax.all_to_all(
            forecast.reshape(MEMBERS, SLOT, LANES), MEMBER, 0, 0, tiled=True
        )
    with jax.named_scope("score"):
        (pred_grads,) = call(
            score_kernel, [((MEMBERS, SLOT, LANES), bf16)], [], 8, 10_000_000, forecasts, truth, area
        )
    with jax.named_scope("gradients_over_member"):
        pred_grad = lax.all_to_all(pred_grads, MEMBER, 0, 0, tiled=True).reshape(ROWS, LANES)
    with jax.named_scope("upstream"):
        upd, scaled, g0, g1, message, loss_part = call(
            upstream_kernel,
            [((ROWS, WIDTH), f32)] + [((ROWS, INNER), bf16)] * 3 + [((ROWS, LANES), bf16), ((8, LANES), f32)],
            [((ROWS, INNER), f32)],
            16,
            500_000_000,
            place, pred_grad, decoder, wa, wb, mixed, total, reach_row,
        )
    with jax.named_scope("gradient_halo"):
        message_low, message_high = both_ways(message)
    with jax.named_scope("query_gradients"):
        (qgrad,) = call(
            query_kernel,
            [((ROWS, INNER), f32)],
            [((2, TILE, WINDOW), f32)],
            12,
            4_000_000_000,
            place, q, k, v, g0, g1, reach_row,
        )
    with jax.named_scope("loss_over_node"):
        (loss_part,) = call(
            pair_kernel, [((8, LANES), f32)], [], 4, 10_000, place, loss_part, message_low, message_high
        )
        loss_part = lax.ppermute(loss_part, EVERY, loss_route())
    with jax.named_scope("backward"):
        (qkv_grad,) = call(
            backward_kernel,
            [((ROWS, 3 * INNER), bf16)],
            [((EXT, INNER), bf16)] * 3
            + [((8, EXT), jnp.int32)]
            + [((2, TILE, WINDOW), f32), ((ROWS, INNER), f32), ((ROWS, WIDTH), f32)],
            24,
            4_000_000_000,
            place, message_low, message_high, decoder, wa, wb, q, k, v, scaled, g0, g1, reach_row,
            qgrad, unit, factor,
        )
    with jax.named_scope("hidden_gradient"):
        noise, send = call(
            hidden_kernel,
            [((ROWS, WIDTH), f32), ((MEMBERS, HEAD + 16, ROWS), bf16)],
            [((ROWS, WIDTH), f32)],
            16,
            1_000_000_000,
            place, qkv_grad, wa, wb, latent_own, pert, gain, upd, loss_part,
        )
    with jax.named_scope("latent_gradient_over_member"):
        received = lax.all_to_all(send, MEMBER, 0, 0, tiled=True)
    with jax.named_scope("finish"):
        latent_grad, loss = call(
            functools.partial(finish_kernel, 1.0 / (MEMBERS * node_total * VARS)),
            [((HEAD, ROWS), f32), ((1, 1), f32)], [], 8, 10_000_000, received,
        )
    return (loss.reshape(()), latent_grad.T, noise[None])


def solution(mesh):
    fine = Mesh(mesh.devices.reshape(4, 2, 2, 16, 2), EVERY)
    placed = (
        P(NODE, MEMBER),
        P(MEMBER, NODE, None),
        P(),
        P(NODE, None),
        P(NODE, None),
        P(),
        P(None, NODE),
        P(NODE),
        P(NODE),
    )
    return jax.shard_map(
        shards,
        mesh=fine,
        in_specs=placed,
        out_specs=(P(), P(NODE, MEMBER), P(MEMBER, NODE, None)),
        check_vma=False,
    )
```
